256 devices in a mesh: expert: 64 (over z, x, core), tensor: 4 (over y).
Axes of the slice: x: 4, y: 4, z: 8, core: 2. Of those that a mesh axis runs over, the one named last changes fastest.
Arguments:
- tokens: bfloat16 [8192, 4096], P('expert'), may hold values from -6 to 6
- expert_ids: int32 [8192, 8], P('expert'), may hold values from 0 to 63, all different within a row; in each aligned block of 128 rows (0 to 127, 128 to 255, ...) at most 24 rows name the same one
- gate_codes: int32 [8192, 8], P('expert'), may hold values from 1 to 256
- w_gate: bfloat16 [64, 4096, 1536], P('expert', None, 'tensor'), may hold values from -0.09375 to 0.09375
- w_up: bfloat16 [64, 4096, 1536], P('expert', None, 'tensor'), may hold values from -0.09375 to 0.09375
- w_down: bfloat16 [64, 1536, 4096], P('expert', 'tensor'), may hold values from -0.15625 to 0.15625
Outputs:
- mixed: bfloat16 [8192, 4096], P('expert', 'tensor')
The draws below stay inside these ranges and needn't reach their ends.
Inputs may be any that keep to these rules, and one draw needn't show every extreme that they name: `expert_ids`: each row names 8 different experts; within each aligned block of 128 rows no expert is named by more than 24 rows, a bound that some block reaches.
All inputs are finite; a program needn't handle non-finite values.
Results may differ from the reference program's by a relative error of at most 0.015.
Values may be sent and summed in bfloat16 or wider, within the bound.
No kernel may reach another device: no remote copies, remote signals or barrier semaphores. Data moves between devices by JAX's collectives and lax.ppermute only.
A program may use at most 128 MiB of HBM per device.

```python
import math
import jax
import jax.numpy as jnp
import numpy as np
from jax import lax

D = 4096
FF = 1536
TOP = 8
TOK_DEV = 128
EXPERTS = 64
CAP = 24
TOKENS = 8192
N_EXPERT = 64
N_TENSOR = 4


def plant(array, key, smallest, high):
    longest = array.shape.index(max(array.shape))
    spots = []
    for shift in (0, 1):
        where = [jax.random.randint(jax.random.fold_in(key, axis), (), 0, length) for axis, length in enumerate(array.shape)]
        where[longest] = (where[longest] + shift) % array.shape[longest]
        spots.append(tuple(where))
    return array.at[spots[0]].set(smallest).at[spots[1]].set(high)


def shard_levels(key, dims, split, least, top_value):
    def one(dim, shards_of):
        draws = jax.random.uniform(jax.random.fold_in(jax.random.fold_in(key, 6), dim), (shards_of,), jnp.float32, least / len(split), top_value / len(split))
        return jnp.repeat(jnp.exp(draws), dims[dim] // shards_of).reshape((-1,) + (1,) * (len(dims) - dim - 1))

    loudness = one(*split[0])
    for cut in split[1:]:
        loudness = loudness * one(*cut)
    return loudness


def routed_block(stream_key, own, number, rows, amount, top, most, lean):
    sequence = jax.random.permutation(stream_key, amount)
    crowded, usual = shares(amount, rows * top, most, lean, True), shares(amount, rows * top, most, lean, False)
    places = jnp.arange(amount)

    def named(tallies, rotation):
        used = int((tallies > 0).sum())
        fixed = max(1, used // 4)
        moved = fixed + (places - fixed + rotation * (used - fixed)) % max(1, amount - fixed)
        return jnp.zeros((amount,), jnp.int32).at[sequence[jnp.where(places < fixed, places, moved)]].set(jnp.asarray(tallies, jnp.int32))

    tallies = jnp.where(number % 4 == 0, named(crowded, number // 4), named(usual, number - number // 4 - 1))
    mixed = jax.random.permutation(jax.random.fold_in(own, 3), amount)
    source_of, taker = mixed[0:amount // 2 * 2:2], mixed[1:amount // 2 * 2:2]
    slack = jnp.minimum(tallies[source_of] - 1, most - tallies[taker]) // 2
    slack = jnp.where((source_of == sequence[0]) | (taker == sequence[0]) | (tallies[taker] == 0), 0, jnp.maximum(slack, 0))
    moved = jax.random.randint(jax.random.fold_in(own, 4), (amount // 2,), 0, 1 << 20) % (slack + 1)
    tallies = tallies.at[source_of].add(-moved).at[taker].add(moved)
    members = jnp.searchsorted(jnp.cumsum(tallies), jnp.arange(rows * top), side="right").astype(jnp.int32)
    listing = members.reshape(top, rows).T
    listing = listing[jax.random.permutation(jax.random.fold_in(own, 1), rows)]
    rotation = jax.random.randint(jax.random.fold_in(own, 2), (rows, 1), 0, top)
    return jnp.take_along_axis(listing, (jnp.arange(top)[None, :] + rotation) % top, axis=1)


def shares(amount, total, limit, slope, full):
    loads = [(1 << 20) // math.isqrt(standing ** slope) + 1 for standing in range(1, amount + 1)]
    largest = limit if full else min(limit, max(-(-total // amount), total * loads[0] // sum(loads)))
    least = 1 if total - largest >= amount - 1 else 0
    counts, rest = [largest] + [least] * (amount - 1), total - largest - least * (amount - 1)
    while rest > 0:
        movable = [i for i in range(1, amount) if counts[i] < largest] or [i for i in range(1, amount) if counts[i] < limit]
        whole, remaining = sum([loads[i] for i in movable]), rest
        for i in movable:
            more = min(limit - counts[i], max(1, remaining * loads[i] // whole), rest)
            counts[i] = counts[i] + more
            rest = rest - more
    return np.array(counts)


def centred(own_key, dims, spread, reach, cuts=(), held_as=jnp.bfloat16):
    entries = jax.random.normal(own_key, dims, jnp.float32) * spread
    if len(cuts) > 0:
        entries = shard_levels(own_key, dims, cuts, -0.22, 0.18) * entries
    return jnp.clip(entries, min=-reach, max=reach).astype(held_as)


def setup_inputs(seed: int = 0) -> dict:
    seeds = jax.random.split(jax.random.key(seed), 7)
    tokens = centred(seeds[0], (TOKENS, D), 1.0, 6.0, ((0, 64),))
    expert_ids_keys = jax.random.split(jax.random.fold_in(seeds[1], 1), TOKENS // TOK_DEV)
    expert_ids_turns = jax.random.permutation(jax.random.fold_in(seeds[1], 3), TOKENS // TOK_DEV)
    expert_ids = jax.vmap(lambda own, number: routed_block(jax.random.fold_in(seeds[1], 2), own, number, TOK_DEV, EXPERTS, TOP, CAP, 2))(expert_ids_keys, expert_ids_turns).reshape((TOKENS, TOP))
    gate_codes = plant(jax.random.randint(seeds[2], (TOKENS, TOP), 1, 257), jax.random.fold_in(seeds[2], 1), 1, 256).astype(jnp.int32)
    w_gate = centred(seeds[3], (EXPERTS, D, FF), D ** -0.5, 0.09375, ((0, 64), (2, 4)))
    w_up = centred(seeds[4], (EXPERTS, D, FF), D ** -0.5, 0.09375, ((0, 64), (2, 4)))
    w_down = centred(seeds[5], (EXPERTS, FF, D), FF ** -0.5, 0.15625, ((0, 64), (1, 4)))
    return {"tokens": tokens, "expert_ids": expert_ids, "gate_codes": gate_codes, "w_gate": w_gate, "w_up": w_up, "w_down": w_down}


def reference(tokens, expert_ids, gate_codes, w_gate, w_up, w_down):
    groups = N_EXPERT
    rows = TOK_DEV
    ids = expert_ids.reshape(groups, rows * TOP)
    onehot = (ids[:, :, None] == jnp.arange(EXPERTS, dtype=jnp.int32)[None, None, :]).astype(jnp.int32)
    before = jnp.sum((jnp.cumsum(onehot, axis=1) - onehot) * onehot, axis=2).astype(jnp.int32)
    source = jnp.arange(groups, dtype=jnp.int32)[:, None]
    slot = (ids * (groups * CAP) + source * CAP + before).reshape(-1)
    token = (source * rows + jnp.arange(rows * TOP, dtype=jnp.int32)[None, :] // TOP).reshape(-1)
    table = jnp.full((EXPERTS * groups * CAP,), -1, jnp.int32).at[slot].set(token)
    table = table.reshape(EXPERTS, groups * CAP)
    scales = gate_codes.astype(jnp.float32).reshape(-1) / 256.0
    weight_of = jnp.zeros((EXPERTS * groups * CAP,), jnp.float32).at[slot].set(scales)
    weight_of = weight_of.reshape(EXPERTS, groups * CAP)
    quarter = FF // N_TENSOR

    def one_expert(total, items):
        index, weights, wg, wu, wd = items
        valid = index >= 0
        safe = jnp.maximum(index, 0)
        picked = jnp.where(valid[:, None], tokens[safe], jnp.zeros((), jnp.bfloat16)).astype(jnp.bfloat16)
        gate = jnp.dot(picked, wg, preferred_element_type=jnp.float32)
        up = jnp.dot(picked, wu, preferred_element_type=jnp.float32)
        hidden = (jax.nn.silu(gate) * up).astype(jnp.bfloat16)
        summed = jnp.zeros((picked.shape[0], D), jnp.float32)
        for q in range(N_TENSOR):
            piece = jnp.dot(hidden[:, q * quarter:(q + 1) * quarter], wd[q * quarter:(q + 1) * quarter], preferred_element_type=jnp.float32)
            summed = summed + piece.astype(jnp.bfloat16).astype(jnp.float32)
        expert_out = summed.astype(jnp.bfloat16).astype(jnp.float32)
        total = total.at[safe].add(expert_out * weights[:, None])
        return total, None

    total = jnp.zeros((groups * rows, D), jnp.float32)
    total, _ = lax.scan(one_expert, total, (table, weight_of, w_gate, w_up, w_down))
    return total.astype(jnp.bfloat16)
```

```python
import jax
import jax.numpy as jnp
from jax import lax
from jax.sharding import PartitionSpec as P

CAPACITY = 24
CHUNKS = ((0, 8), (8, 8), (16, 8))


def neighbours(shift, size):
    return [(i, (i + shift) % size) for i in range(size)]


def ring_gather(piece, axis):
    size = lax.axis_size(axis)
    half = piece.shape[0] // 2
    before = lax.ppermute(piece, axis, neighbours(1, size))
    after = lax.ppermute(piece, axis, neighbours(-1, size))
    far_top = lax.ppermute(before[:half], axis, neighbours(1, size))
    far_bottom = lax.ppermute(after[half:], axis, neighbours(-1, size))
    return piece, before, after, jnp.concatenate([far_top, far_bottom], axis=0)


def by_ring(array, length, axis):
    me = lax.axis_index(axis)
    size = lax.axis_size(axis)
    return [
        lax.dynamic_slice_in_dim(array, lax.rem(me + shift, size) * length, length, 0)
        for shift in (0, size - 1, 1, 2)
    ]


def shards(tokens, expert_ids, gate_codes, w_gate, w_up, w_down):
    groups = lax.axis_size("expert")
    parts = lax.axis_size("tensor")
    me = lax.axis_index("tensor")
    rows, width = tokens.shape
    quarter = width // parts
    units = w_gate.shape[2]

    named = expert_ids[:, :, None] == jnp.arange(groups, dtype=jnp.int32)[None, None, :]
    member = jnp.any(named, axis=1)
    weight = jnp.sum(jnp.where(named, gate_codes[:, :, None], 0), axis=1).astype(jnp.float32) / 256.0
    earlier = (jnp.arange(rows)[:, None] > jnp.arange(rows)[None, :]).astype(jnp.bfloat16)
    slot = jnp.dot(earlier, member.astype(jnp.bfloat16), preferred_element_type=jnp.float32).astype(jnp.int32)
    slot = jnp.where(member, slot, -1).T
    weight = weight.T

    mine = lax.dynamic_slice_in_dim(tokens, me * quarter, quarter, 1)
    picks, sent = [], []
    for first, count in CHUNKS:
        pick = slot[:, None, :] == (first + jnp.arange(count, dtype=jnp.int32))[None, :, None]
        picks.append(pick)
        chosen = pick.astype(jnp.bfloat16).reshape(groups * count, rows)
        send = jnp.dot(chosen, mine, preferred_element_type=jnp.float32).astype(jnp.bfloat16)
        sent.append(send.reshape(groups, count, quarter))

    w_in = jnp.concatenate([w_gate[0], w_up[0]], axis=1)
    w_in = by_ring(w_in, quarter, "tensor")
    w_out = lax.all_to_all(w_down[0], "tensor", split_axis=1, concat_axis=0, tiled=True)
    w_out = by_ring(w_out, units, "tensor")

    mixed = jnp.zeros((rows, quarter), jnp.float32)
    for (first, count), pick, send in zip(CHUNKS, picks, sent):
        received = lax.all_to_all(send, "expert", split_axis=0, concat_axis=0, tiled=True)
        pieces = ring_gather(received.reshape(groups * count, quarter), "tensor")
        both = sum(jnp.dot(x, w, preferred_element_type=jnp.float32) for x, w in zip(pieces, w_in))
        gate, up = both[:, :units], both[:, units:]
        hidden = (jax.nn.silu(gate) * up).astype(jnp.bfloat16)
        pieces = ring_gather(hidden, "tensor")
        out = sum(jnp.dot(x, w, preferred_element_type=jnp.float32) for x, w in zip(pieces, w_out))
        out = out.astype(jnp.bfloat16).reshape(groups, count, quarter)
        returned = lax.all_to_all(out, "expert", split_axis=0, concat_axis=0, tiled=True)
        scale = jnp.where(pick, weight[:, None, :], 0.0).astype(jnp.bfloat16).reshape(groups * count, rows)
        mixed = mixed + lax.dot_general(
            scale, returned.reshape(groups * count, quarter), (((0,), (0,)), ((), ())),
            preferred_element_type=jnp.float32,
        )
    return mixed.astype(jnp.bfloat16)


def solution(mesh):
    placed = (
        P("expert", None),
        P("expert", None),
        P("expert", None),
        P("expert", None, "tensor"),
        P("expert", None, "tensor"),
        P("expert", "tensor", None),
    )
    return jax.shard_map(
        shards, mesh=mesh, in_specs=placed, out_specs=P("expert", "tensor"), check_vma=False
    )
```

```python
import jax
import jax.numpy as jnp
from jax import lax
from jax.sharding import PartitionSpec as P

CAPACITY = 24
CHUNKS = ((0, 8), (8, 8), (16, 8))


def neighbours(shift, size):
    return [(i, (i + shift) % size) for i in range(size)]


def after(value, *earlier):
    return lax.optimization_barrier((value, earlier))[0]


def ring_gather(piece, axis):
    size = lax.axis_size(axis)
    half = piece.shape[0] // 2
    last = lax.ppermute(piece, axis, neighbours(1, size))
    following = lax.ppermute(piece, axis, neighbours(-1, size))
    far_top = lax.ppermute(last[:half], axis, neighbours(1, size))
    far_bottom = lax.ppermute(following[half:], axis, neighbours(-1, size))
    return piece, last, following, jnp.concatenate([far_top, far_bottom], axis=0)


def stack(*blocks):
    return jnp.concatenate(blocks, axis=0)


def both_ways(down, up, axis):
    size = lax.axis_size(axis)
    return (
        lax.ppermute(down, axis, neighbours(1, size)),
        lax.ppermute(up, axis, neighbours(-1, size)),
    )


def by_ring(array, length, axis):
    me = lax.axis_index(axis)
    size = lax.axis_size(axis)
    return [
        lax.dynamic_slice_in_dim(array, lax.rem(me + shift, size) * length, length, 0)
        for shift in (0, size - 1, 1, 2)
    ]


def shards(tokens, expert_ids, gate_codes, w_gate, w_up, w_down):
    groups = lax.axis_size("expert")
    parts = lax.axis_size("tensor")
    me = lax.axis_index("tensor")
    rows, width = tokens.shape
    quarter = width // parts
    units = w_gate.shape[2]

    named = expert_ids[:, :, None] == jnp.arange(groups, dtype=jnp.int32)[None, None, :]
    member = jnp.any(named, axis=1)
    weight = jnp.sum(jnp.where(named, gate_codes[:, :, None], 0), axis=1).astype(jnp.float32) / 256.0
    earlier = (jnp.arange(rows)[:, None] > jnp.arange(rows)[None, :]).astype(jnp.bfloat16)
    slot = jnp.dot(earlier, member.astype(jnp.bfloat16), preferred_element_type=jnp.float32).astype(jnp.int32)
    slot = jnp.where(member, slot, -1).T
    weight = weight.T

    mine = lax.dynamic_slice_in_dim(tokens, me * quarter, quarter, 1)
    picks, sent = [], []
    for first, count in CHUNKS:
        pick = slot[:, None, :] == (first + jnp.arange(count, dtype=jnp.int32))[None, :, None]
        picks.append(pick)
        chosen = pick.astype(jnp.bfloat16).reshape(groups * count, rows)
        send = jnp.dot(chosen, mine, preferred_element_type=jnp.float32).astype(jnp.bfloat16)
        sent.append(send.reshape(groups, count, quarter))

    w_in = jnp.concatenate([w_gate[0], w_up[0]], axis=1)
    w_in = by_ring(w_in, quarter, "tensor")

    def dispatch(send):
        received = lax.all_to_all(send, "expert", split_axis=0, concat_axis=0, tiled=True)
        return received.reshape(-1, quarter)

    def columns_of(shift):
        return lax.dynamic_slice_in_dim(w_down[0], lax.rem(me + shift, parts) * quarter, quarter, 1)

    top = units // 2
    opposite = columns_of(2)
    down, up = both_ways(
        stack(columns_of(1), opposite[:top]), stack(columns_of(parts - 1), opposite[top:]), "tensor"
    )
    far = both_ways(down[units:], up[units:], "tensor")
    w_out = [columns_of(0), down[:units], up[:units], stack(*far)]

    received = [after(dispatch(sent[0]), down, up)]
    firsts, fars = [], []
    for step in range(len(CHUNKS) + 1):
        parts_down, parts_up = [], []
        if step < len(CHUNKS):
            parts_down.append(received[step])
            parts_up.append(received[step])
        if step > 0:
            half = firsts[step - 1][0].shape[0] // 2
            parts_down.append(firsts[step - 1][0][:half])
            parts_up.append(firsts[step - 1][1][half:])
        arrived = both_ways(stack(*parts_down), stack(*parts_up), "tensor")
        length = received[step].shape[0] if step < len(CHUNKS) else 0
        if step < len(CHUNKS):
            firsts.append((arrived[0][:length], arrived[1][:length]))
        if step > 0:
            fars.append(stack(arrived[0][length:], arrived[1][length:]))
        if step + 1 < len(CHUNKS):
            following = dispatch(after(sent[step + 1], *(arrived_before if step else (down, up))))
            received.append(following if step else after(following, *far))
        arrived_before = arrived
    gathered = [(own, *first, far) for own, first, far in zip(received, firsts, fars)]

    previous = returned = None
    mixed = jnp.zeros((rows, quarter), jnp.float32)
    for (first, count), pick, pieces in zip(CHUNKS, picks, gathered):
        both = sum(jnp.dot(x, w, preferred_element_type=jnp.float32) for x, w in zip(pieces, w_in))
        gate, up = both[:, :units], both[:, units:]
        hidden = (jax.nn.silu(gate) * up).astype(jnp.bfloat16)
        if previous is not None:
            hidden = after(hidden, *previous)
        pieces = ring_gather(hidden, "tensor")
        previous = pieces[3:]
        out = sum(jnp.dot(x, w, preferred_element_type=jnp.float32) for x, w in zip(pieces, w_out))
        out = out.astype(jnp.bfloat16).reshape(groups, count, quarter)
        if returned is not None:
            out = after(out, returned)
        returned = lax.all_to_all(out, "expert", split_axis=0, concat_axis=0, tiled=True)
        scale = jnp.where(pick, weight[:, None, :], 0.0).astype(jnp.bfloat16).reshape(groups * count, rows)
        mixed = mixed + lax.dot_general(
            scale, returned.reshape(groups * count, quarter), (((0,), (0,)), ((), ())),
            preferred_element_type=jnp.float32,
        )
    return mixed.astype(jnp.bfloat16)


def solution(mesh):
    placed = (
        P("expert", None),
        P("expert", None),
        P("expert", None),
        P("expert", None, "tensor"),
        P("expert", None, "tensor"),
        P("expert", "tensor", None),
    )
    return jax.shard_map(
        shards, mesh=mesh, in_specs=placed, out_specs=P("expert", "tensor"), check_vma=False
    )
```

```python
import jax
import jax.numpy as jnp
from jax import lax
from jax.sharding import PartitionSpec as P

CHUNKS = ((0, 8), (8, 8), (16, 8))
PLANE = 8


def neighbours(shift, size):
    return [(i, (i + shift) % size) for i in range(size)]


def after(value, *earlier):
    return lax.optimization_barrier((value, earlier))[0]


def ring_gather(piece, axis):
    size = lax.axis_size(axis)
    half = piece.shape[0] // 2
    last = lax.ppermute(piece, axis, neighbours(1, size))
    following = lax.ppermute(piece, axis, neighbours(-1, size))
    far_top = lax.ppermute(last[:half], axis, neighbours(1, size))
    far_bottom = lax.ppermute(following[half:], axis, neighbours(-1, size))
    return piece, last, following, jnp.concatenate([far_top, far_bottom], axis=0)


def stack(*blocks):
    return jnp.concatenate(blocks, axis=0)


def both_ways(down, up, axis):
    size = lax.axis_size(axis)
    return (
        lax.ppermute(down, axis, neighbours(1, size)),
        lax.ppermute(up, axis, neighbours(-1, size)),
    )


def shards(tokens, expert_ids, gate_codes, w_gate, w_up, w_down):
    groups = lax.axis_size("expert")
    parts = lax.axis_size("tensor")
    me = lax.axis_index("tensor")
    plane = lax.axis_index("expert") // PLANE
    planes = groups // PLANE
    rows, width = tokens.shape
    half, quarter = width // 2, width // parts
    units = w_gate.shape[2]
    in_plane = [[z * PLANE + j for j in range(PLANE)] for z in range(planes)]
    in_column = [[z * PLANE + j for z in range(planes)] for j in range(PLANE)]

    named = expert_ids[:, :, None] == jnp.arange(groups, dtype=jnp.int32)[None, None, :]
    member = jnp.any(named, axis=1)
    weight = jnp.sum(jnp.where(named, gate_codes[:, :, None], 0), axis=1).astype(jnp.float32) / 256.0
    earlier = (jnp.arange(rows)[:, None] > jnp.arange(rows)[None, :]).astype(jnp.bfloat16)
    slot = jnp.dot(earlier, member.astype(jnp.bfloat16), preferred_element_type=jnp.float32).astype(jnp.int32)
    slot = jnp.where(member, slot, -1).T
    weight = weight.T

    def ring(value, shift):
        return lax.ppermute(value, "expert", [(i, (i + shift * PLANE) % groups) for i in range(groups)])

    def place(everything, block, shift):
        return lax.dynamic_update_slice_in_dim(everything, block, lax.rem(plane + shift, planes) * rows, 0)

    parity = lax.rem(me, 2)
    mine = lax.dynamic_slice_in_dim(tokens, parity * half, half, 1)
    everything = place(jnp.zeros((planes * rows, half), jnp.bfloat16), mine, 0)
    down = up = mine
    for step in range(1, planes // 2 + 1):
        down = ring(down, 1)
        everything = place(everything, down, planes - step)
        if 2 * step < planes:
            up = ring(up, -1)
            everything = place(everything, up, step)
    slots = lax.all_to_all(
        slot.reshape(planes, PLANE, rows), "expert", split_axis=0, concat_axis=0, tiled=True,
        axis_index_groups=in_column,
    )

    w_in = stack(*(
        jnp.concatenate(
            [lax.dynamic_slice_in_dim(w[0], start * half, half, 0) for w in (w_gate, w_up)], axis=1
        )
        for start in (parity, 1 - parity)
    ))
    w_in = (w_in[:half], w_in[half:half + quarter], w_in[half + quarter:])

    def columns_of(shift):
        return lax.dynamic_slice_in_dim(w_down[0], lax.rem(me + shift, parts) * quarter, quarter, 1)

    top = units // 2
    opposite = columns_of(2)
    down, up = both_ways(
        stack(columns_of(1), opposite[:top]), stack(columns_of(parts - 1), opposite[top:]), "tensor"
    )
    far = both_ways(down[units:], up[units:], "tensor")
    w_out = [columns_of(0), down[:units], up[:units], stack(*far)]

    received, arrived = [], []
    own_plane = jnp.arange(planes)[None, :, None, None, None] == jnp.arange(planes)[None, None, None, :, None]
    for first, count in CHUNKS:
        place_of = (first + jnp.arange(count, dtype=jnp.int32))[None, None, :, None, None]
        pick = own_plane & (slots.transpose(1, 0, 2)[:, None, None, :, :] == place_of)
        pick = pick.astype(jnp.bfloat16).reshape(groups * count, planes * rows)
        send = jnp.dot(pick, everything, preferred_element_type=jnp.float32).astype(jnp.bfloat16)
        send = after(send, *(received[-1:] or far))
        got = lax.all_to_all(
            send.reshape(PLANE, planes * count, half), "expert", split_axis=0, concat_axis=0, tiled=True,
            axis_index_groups=in_plane,
        )
        received.append(got.reshape(groups * count, half))

    mixed = jnp.zeros((rows, quarter), jnp.float32)
    previous = returned = None
    hiddens = []
    for step, (first, count) in enumerate(CHUNKS):
        own = received[step]
        if step:
            own = after(own, *arrived[step - 1])
        if step >= 2:
            own = after(own, *hiddens[step - 2][3:])
        arrived.append(both_ways(own[:, :quarter], own[:, quarter:], "tensor"))
        both = sum(jnp.dot(x, w, preferred_element_type=jnp.float32) for x, w in zip((own, *arrived[step]), w_in))
        gate, up = both[:, :units], both[:, units:]
        hidden = (jax.nn.silu(gate) * up).astype(jnp.bfloat16)
        hidden = hidden.reshape(PLANE, planes, count, units).transpose(1, 0, 2, 3).reshape(groups * count, units)
        if step:
            hidden = after(hidden, *hiddens[step - 1][3:])
        hiddens.append(ring_gather(hidden, "tensor"))

    for step, (first, count) in enumerate(CHUNKS):
        out = sum(jnp.dot(x, w, preferred_element_type=jnp.float32) for x, w in zip(hiddens[step], w_out))
        out = out.astype(jnp.bfloat16).reshape(groups, count, quarter)
        out = after(out, received[-1] if returned is None else returned)
        returned = lax.all_to_all(out, "expert", split_axis=0, concat_axis=0, tiled=True)
        pick = slot[:, None, :] == (first + jnp.arange(count, dtype=jnp.int32))[None, :, None]
        scale = jnp.where(pick, weight[:, None, :], 0.0).astype(jnp.bfloat16).reshape(groups * count, rows)
        mixed = mixed + lax.dot_general(
            scale, returned.reshape(groups * count, quarter), (((0,), (0,)), ((), ())),
            preferred_element_type=jnp.float32,
        )
    return mixed.astype(jnp.bfloat16)


def solution(mesh):
    placed = (
        P("expert", None),
        P("expert", None),
        P("expert", None),
        P("expert", None, "tensor"),
        P("expert", None, "tensor"),
        P("expert", "tensor", None),
    )
    return jax.shard_map(
        shards, mesh=mesh, in_specs=placed, out_specs=P("expert", "tensor"), check_vma=False
    )
```

```python
import functools

import jax
import jax.numpy as jnp
from jax import lax
from jax.experimental import pallas as pl
from jax.experimental.pallas import tpu as pltpu
from jax.sharding import PartitionSpec as P

CHUNKS = ((0, 8), (8, 8), (16, 8))
PLANE = 8


def neighbours(shift, size):
    return [(i, (i + shift) % size) for i in range(size)]


def after(value, *earlier):
    return lax.optimization_barrier((value, earlier))[0]


def ring_gather(piece, axis):
    size = lax.axis_size(axis)
    half = piece.shape[0] // 2
    last = lax.ppermute(piece, axis, neighbours(1, size))
    following = lax.ppermute(piece, axis, neighbours(-1, size))
    far_top = lax.ppermute(last[:half], axis, neighbours(1, size))
    far_bottom = lax.ppermute(following[half:], axis, neighbours(-1, size))
    return piece, last, following, far_top, far_bottom


def stack(*blocks):
    return jnp.concatenate(blocks, axis=0)


def both_ways(down, up, axis):
    size = lax.axis_size(axis)
    return (
        lax.ppermute(down, axis, neighbours(1, size)),
        lax.ppermute(up, axis, neighbours(-1, size)),
    )


def select_kernel(first, count, slots_ref, rows_ref, out_ref):
    blocks, experts, length = slots_ref.shape
    spot = lax.broadcasted_iota(jnp.int32, (experts, blocks * count, length), 1)
    picks = []
    for b in range(blocks):
        slot = slots_ref[b] - first
        slot = jnp.where((slot >= 0) & (slot < count), slot + b * count, -1)
        pick = jnp.where(spot == slot[:, None, :], 1.0, 0.0).reshape(experts * blocks * count, length)
        picks.append(pick.astype(jnp.bfloat16))
    chosen = jnp.dot(jnp.concatenate(picks, axis=1), rows_ref[...], preferred_element_type=jnp.float32)
    out_ref[...] = chosen.astype(jnp.bfloat16).reshape(out_ref.shape)


def select(slots, everything, first, count):
    planes, experts, length = slots.shape
    width = everything.shape[1]
    blocks = max(1, 16 // count)
    return pl.pallas_call(
        functools.partial(select_kernel, first, count),
        out_shape=jax.ShapeDtypeStruct((experts, planes * count, width), jnp.bfloat16),
        grid=(planes // blocks,),
        in_specs=[
            pl.BlockSpec((blocks, experts, length), lambda b: (b, 0, 0)),
            pl.BlockSpec((blocks * length, width), lambda b: (b, 0)),
        ],
        out_specs=pl.BlockSpec((experts, blocks * count, width), lambda b: (0, b, 0)),
        cost_estimate=pl.CostEstimate(
            flops=2 * experts * planes * count * blocks * length * width,
            bytes_accessed=2 * width * planes * (length + experts * count), transcendentals=0,
        ),
    )(slots, everything)


def hidden_kernel(piece, first_ref, own_ref, last_ref, next_ref, gate_ref, up_ref, out_ref, gate, up):
    step = pl.program_id(0)

    def add(x):
        for total, w in ((gate, gate_ref), (up, up_ref)):
            part = jnp.dot(x, w[...], preferred_element_type=jnp.float32)
            total[...] = jnp.where(step == 0, part, total[...] + part)

    @pl.when(step < 2)
    def _():
        add(own_ref[...])

    @pl.when(step == 2)
    def _():
        add(last_ref[...])

    @pl.when(step == 3)
    def _():
        add(next_ref[...])
        outer, inner, count = piece
        for b in range(inner):
            rows = [(j * inner + b) * count for j in range(outer)]
            g = jnp.concatenate([gate[r:r + count] for r in rows], axis=0)
            u = jnp.concatenate([up[r:r + count] for r in rows], axis=0)
            block = g / (1.0 + jnp.exp(-g)) * u
            out_ref[b * outer * count:(b + 1) * outer * count] = block.astype(jnp.bfloat16)


def hidden_of(parity, own, last, following, w_gate, w_up, piece):
    length, quarter = last.shape
    units = w_gate.shape[1]

    def weight_block(k, first):
        return lax.rem(first[0] * 2 + k, 4), 0

    return pl.pallas_call(
        functools.partial(hidden_kernel, piece),
        out_shape=jax.ShapeDtypeStruct((length, units), jnp.bfloat16),
        grid_spec=pltpu.PrefetchScalarGridSpec(
            num_scalar_prefetch=1,
            grid=(4,),
            in_specs=[
                pl.BlockSpec((length, quarter), lambda k, first: (0, jnp.minimum(k, 1))),
                pl.BlockSpec((length, quarter), lambda k, first: (0, 0)),
                pl.BlockSpec((length, quarter), lambda k, first: (0, 0)),
                pl.BlockSpec((quarter, units), weight_block),
                pl.BlockSpec((quarter, units), weight_block),
            ],
            out_specs=pl.BlockSpec((length, units), lambda k, first: (0, 0)),
            scratch_shapes=[pltpu.VMEM((length, units), jnp.float32)] * 2,
        ),
        compiler_params=pltpu.CompilerParams(vmem_limit_bytes=32 << 20),
        cost_estimate=pl.CostEstimate(
            flops=16 * length * quarter * units, bytes_accessed=8 * quarter * (length + 2 * units),
            transcendentals=length * units,
        ),
    )(parity, own, last, following, w_gate, w_up)


def down_kernel(me_ref, own_ref, last_ref, next_ref, top_ref, bottom_ref, w_own, w_last, w_next, w_far, out_ref):
    def product(far_ref):
        total = jnp.dot(own_ref[...], w_own[...], preferred_element_type=jnp.float32)
        for x, w in ((last_ref, w_last), (next_ref, w_next), (far_ref, w_far)):
            total = total + jnp.dot(x[...], w[...], preferred_element_type=jnp.float32)
        out_ref[...] = total.astype(jnp.bfloat16)

    @pl.when(pl.program_id(0) == 0)
    def _():
        product(top_ref)

    @pl.when(pl.program_id(0) == 1)
    def _():
        product(bottom_ref)


def down_of(me, pieces, weights):
    own, last, following, top, bottom = pieces
    length, units = own.shape
    half = length // 2
    w_down, w_last, w_next, w_far = weights
    quarter = w_far.shape[1]
    rows = pl.BlockSpec((half, units), lambda i, me: (i, 0))
    whole = pl.BlockSpec((half, units), lambda i, me: (0, 0))
    block = pl.BlockSpec((units, quarter), lambda i, me: (0, 0))
    return pl.pallas_call(
        down_kernel,
        out_shape=jax.ShapeDtypeStruct((length, quarter), jnp.bfloat16),
        grid_spec=pltpu.PrefetchScalarGridSpec(
            num_scalar_prefetch=1,
            grid=(2,),
            in_specs=[rows, rows, rows, whole, whole]
            + [pl.BlockSpec((units, quarter), lambda i, me: (0, me[0])), block, block, block],
            out_specs=pl.BlockSpec((half, quarter), lambda i, me: (i, 0)),
        ),
        compiler_params=pltpu.CompilerParams(vmem_limit_bytes=32 << 20),
        cost_estimate=pl.CostEstimate(
            flops=8 * length * units * quarter, bytes_accessed=8 * units * (quarter + length) + 2 * length * quarter,
            transcendentals=0,
        ),
    )(me, own, last, following, top, bottom, w_down, w_last, w_next, w_far)


def shards(tokens, expert_ids, gate_codes, w_gate, w_up, w_down):
    groups = lax.axis_size("expert")
    parts = lax.axis_size("tensor")
    me = lax.axis_index("tensor")
    plane = lax.axis_index("expert") // PLANE
    planes = groups // PLANE
    rows, width = tokens.shape
    half, quarter = width // 2, width // parts
    units = w_gate.shape[2]
    in_plane = [[z * PLANE + j for j in range(PLANE)] for z in range(planes)]
    in_column = [[z * PLANE + j for z in range(planes)] for j in range(PLANE)]

    named = expert_ids[:, :, None] == jnp.arange(groups, dtype=jnp.int32)[None, None, :]
    member = jnp.any(named, axis=1)
    weight = jnp.sum(jnp.where(named, gate_codes[:, :, None], 0), axis=1).astype(jnp.float32) / 256.0
    earlier = (jnp.arange(rows)[:, None] > jnp.arange(rows)[None, :]).astype(jnp.bfloat16)
    slot = jnp.dot(earlier, member.astype(jnp.bfloat16), preferred_element_type=jnp.float32).astype(jnp.int32)
    slot = jnp.where(member, slot, -1).T
    weight = weight.T

    def ring(value, shift):
        return lax.ppermute(value, "expert", [(i, (i + shift * PLANE) % groups) for i in range(groups)])

    def place(everything, block, shift):
        return lax.dynamic_update_slice_in_dim(everything, block, lax.rem(plane + shift, planes) * rows, 0)

    parity = lax.rem(me, 2)
    mine = lax.dynamic_slice_in_dim(tokens, parity * half, half, 1)
    everything = place(jnp.zeros((planes * rows, half), jnp.bfloat16), mine, 0)
    down = up = mine
    for step in range(1, planes // 2 + 1):
        down = ring(down, 1)
        everything = place(everything, down, planes - step)
        if 2 * step < planes:
            up = ring(up, -1)
            everything = place(everything, up, step)
    slots = lax.all_to_all(
        slot.reshape(planes, PLANE, rows), "expert", split_axis=0, concat_axis=0, tiled=True,
        axis_index_groups=in_column,
    )

    def columns_of(shift):
        return lax.dynamic_slice_in_dim(w_down[0], lax.rem(me + shift, parts) * quarter, quarter, 1)

    top = units // 2
    opposite = columns_of(2)
    down, up = both_ways(
        stack(columns_of(1), opposite[:top]), stack(columns_of(parts - 1), opposite[top:]), "tensor"
    )
    far = both_ways(down[units:], up[units:], "tensor")
    w_out = (w_down[0], down, up, stack(*far))

    sends = [select(slots, everything, first, count) for first, count in CHUNKS]
    received, arrived = [], []
    for step, send in enumerate(sends):
        send = after(send, *(received[-1:] or far))
        got = lax.all_to_all(
            send, "expert", split_axis=0, concat_axis=0, tiled=True, axis_index_groups=in_plane
        ).reshape(-1, half)
        received.append(after(got, *sends[1:]) if step == 0 else got)

    mixed = jnp.zeros((rows, quarter), jnp.float32)
    previous = returned = None
    hiddens = []
    for step, (first, count) in enumerate(CHUNKS):
        own = received[step]
        if step:
            own = after(own, *arrived[step - 1])
        if step >= 2:
            own = after(own, *hiddens[step - 2][3:])
        arrived.append(both_ways(own[:, :quarter], own[:, quarter:], "tensor"))
        hidden = hidden_of(
            parity[None], own, *arrived[step], w_gate[0], w_up[0], (PLANE, planes, count)
        )
        if step:
            hidden = after(hidden, *hiddens[step - 1][3:])
        hiddens.append(ring_gather(hidden, "tensor"))

    for step, (first, count) in enumerate(CHUNKS):
        out = down_of(me[None], hiddens[step], w_out).reshape(groups, count, quarter)
        out = after(out, received[-1] if returned is None else returned)
        returned = lax.all_to_all(out, "expert", split_axis=0, concat_axis=0, tiled=True)
        pick = slot[:, None, :] == (first + jnp.arange(count, dtype=jnp.int32))[None, :, None]
        scale = jnp.where(pick, weight[:, None, :], 0.0).astype(jnp.bfloat16).reshape(groups * count, rows)
        mixed = mixed + lax.dot_general(
            scale, returned.reshape(groups * count, quarter), (((0,), (0,)), ((), ())),
            preferred_element_type=jnp.float32,
        )
    return mixed.astype(jnp.bfloat16)


def solution(mesh):
    placed = (
        P("expert", None),
        P("expert", None),
        P("expert", None),
        P("expert", None, "tensor"),
        P("expert", None, "tensor"),
        P("expert", "tensor", None),
    )
    return jax.shard_map(
        shards, mesh=mesh, in_specs=placed, out_specs=P("expert", "tensor"), check_vma=False
    )
```

```python
import functools

import jax
import jax.numpy as jnp
from jax import lax
from jax.experimental import pallas as pl
from jax.experimental.pallas import tpu as pltpu
from jax.sharding import PartitionSpec as P

CHUNKS = ((0, 8), (8, 8), (16, 8))
PLANE = 8


def neighbours(shift, size):
    return [(i, (i + shift) % size) for i in range(size)]


def after(value, *earlier):
    return lax.optimization_barrier((value, earlier))[0]


def ring_gather(piece, axis):
    size = lax.axis_size(axis)
    half = piece.shape[0] // 2
    last = lax.ppermute(piece, axis, neighbours(1, size))
    following = lax.ppermute(piece, axis, neighbours(-1, size))
    far_top = lax.ppermute(last[:half], axis, neighbours(1, size))
    far_bottom = lax.ppermute(following[half:], axis, neighbours(-1, size))
    return piece, last, following, far_top, far_bottom


def stack(*blocks):
    return jnp.concatenate(blocks, axis=0)


def both_ways(down, up, axis):
    size = lax.axis_size(axis)
    return (
        lax.ppermute(down, axis, neighbours(1, size)),
        lax.ppermute(up, axis, neighbours(-1, size)),
    )


def select_kernel(chunks, planes, plane_ref, slots_ref, *refs):
    outs = refs[-len(chunks):]
    parts = (len(refs) - len(outs)) // planes
    experts, length = slots_ref.shape[1:]
    for (first, count), out_ref in zip(chunks, outs):
        group = max(1, 16 // count)
        spot = lax.broadcasted_iota(jnp.int32, (experts, group * count, length), 1)
        for start in range(0, planes, group):
            picks = []
            for b in range(group):
                slot = slots_ref[lax.rem(plane_ref[0] + start + b, planes)] - first
                slot = jnp.where((slot >= 0) & (slot < count), slot + b * count, -1)
                pick = jnp.where(spot == slot[:, None, :], 1.0, 0.0).reshape(experts * group * count, length)
                picks.append(pick.astype(jnp.bfloat16))
            for part in range(parts):
                blocks = refs[part * planes + start:part * planes + start + group]
                width = blocks[0].shape[1]
                chosen = sum(jnp.dot(p, x[...], preferred_element_type=jnp.float32) for p, x in zip(picks, blocks))
                out_ref[:, start * count:(start + group) * count, part * width:(part + 1) * width] = (
                    chosen.astype(jnp.bfloat16).reshape(experts, group * count, width)
                )


def select(plane, slots, parts, chunks):
    planes, experts, length = slots.shape
    blocks = [block for part in parts for block in part]
    width = sum(part[0].shape[1] for part in parts)
    slots_out = sum(count for _, count in chunks) * planes * experts
    return pl.pallas_call(
        functools.partial(select_kernel, chunks, planes),
        out_shape=[jax.ShapeDtypeStruct((experts, planes * count, width), jnp.bfloat16) for _, count in chunks],
        grid_spec=pltpu.PrefetchScalarGridSpec(
            num_scalar_prefetch=1,
            grid=(1,),
            in_specs=[pl.BlockSpec(slots.shape, lambda i, plane: (0, 0, 0))]
            + [pl.BlockSpec(block.shape, lambda i, plane: (0, 0)) for block in blocks],
            out_specs=[
                pl.BlockSpec((experts, planes * count, width), lambda i, plane: (0, 0, 0)) for _, count in chunks
            ],
        ),
        compiler_params=pltpu.CompilerParams(vmem_limit_bytes=20 << 20),
        cost_estimate=pl.CostEstimate(
            flops=4 * slots_out * length * width, bytes_accessed=2 * width * (planes * length + slots_out),
            transcendentals=0,
        ),
    )(plane, slots, *blocks)


def hidden_kernel(inner, count, plane_ref, half_ref, *refs):
    pieces = (len(refs) - 1) // 3
    x_refs, gate_refs, up_refs, out_ref = refs[:pieces], refs[pieces:2 * pieces], refs[2 * pieces:-1], refs[-1]
    outer, rows = x_refs[0].shape[:2]

    def product(w_refs):
        return sum(
            jnp.dot(x[...].reshape(outer * rows, x.shape[2]), w[...], preferred_element_type=jnp.float32)
            for x, w in zip(x_refs, w_refs)
        )

    gate, up = product(gate_refs), product(up_refs)
    hidden = gate / (1.0 + jnp.exp(-gate)) * up
    for b in range(rows // count):
        block = jnp.concatenate(
            [hidden[j * rows + b * count:j * rows + (b + 1) * count] for j in range(outer)], axis=0
        )
        place = lax.rem(plane_ref[0] + pl.program_id(0) * (rows // count) + b, inner) * (outer * count)
        out_ref[pl.ds(pl.multiple_of(place, outer * count), outer * count)] = block.astype(jnp.bfloat16)


def hidden_of(plane, parity, own, last, following, w_gate, w_up, count):
    pieces = [*own, last, following]
    outer, rows, quarter = last.shape
    units = w_gate.shape[1]
    inner = rows // count
    steps = 2

    def weight(width, place):
        return pl.BlockSpec((width, units), lambda i, plane, half: (place(half[0]), 0))

    if len(own) == 1:
        weights = [weight(2 * quarter, lambda h: h)]
    else:
        weights = [weight(quarter, lambda h: 2 * h), weight(quarter, lambda h: 2 * h + 1)]
    weights += [weight(quarter, lambda h: 2 - 2 * h), weight(quarter, lambda h: 3 - 2 * h)]
    return pl.pallas_call(
        functools.partial(hidden_kernel, inner, count),
        out_shape=jax.ShapeDtypeStruct((outer * rows, units), jnp.bfloat16),
        grid_spec=pltpu.PrefetchScalarGridSpec(
            num_scalar_prefetch=2,
            grid=(steps,),
            in_specs=[
                pl.BlockSpec((outer, rows // steps, x.shape[2]), lambda i, plane, half: (0, i, 0)) for x in pieces
            ] + weights * 2,
            out_specs=pl.BlockSpec((outer * rows, units), lambda i, plane, half: (0, 0)),
        ),
        compiler_params=pltpu.CompilerParams(vmem_limit_bytes=60 << 20),
        cost_estimate=pl.CostEstimate(
            flops=16 * outer * rows * quarter * units, bytes_accessed=8 * quarter * (outer * rows + 2 * units),
            transcendentals=outer * rows * units,
        ),
    )(plane, parity, *pieces, *[w_gate] * len(weights), *[w_up] * len(weights))


def down_kernel(me_ref, own_ref, last_ref, next_ref, top_ref, bottom_ref, w_own, w_last, w_next, w_far, out_ref):
    def product(far_ref):
        total = jnp.dot(own_ref[...], w_own[...], preferred_element_type=jnp.float32)
        for x, w in ((last_ref, w_last), (next_ref, w_next), (far_ref, w_far)):
            total = total + jnp.dot(x[...], w[...], preferred_element_type=jnp.float32)
        out_ref[...] = total.astype(jnp.bfloat16)

    @pl.when(pl.program_id(0) == 0)
    def _():
        product(top_ref)

    @pl.when(pl.program_id(0) == 1)
    def _():
        product(bottom_ref)


def down_of(me, pieces, weights):
    own, last, following, top, bottom = pieces
    length, units = own.shape
    half = length // 2
    w_down, w_last, w_next, w_far = weights
    quarter = w_far.shape[1]
    rows = pl.BlockSpec((half, units), lambda i, me: (i, 0))
    whole = pl.BlockSpec((half, units), lambda i, me: (0, 0))
    block = pl.BlockSpec((units, quarter), lambda i, me: (0, 0))
    return pl.pallas_call(
        down_kernel,
        out_shape=jax.ShapeDtypeStruct((length, quarter), jnp.bfloat16),
        grid_spec=pltpu.PrefetchScalarGridSpec(
            num_scalar_prefetch=1,
            grid=(2,),
            in_specs=[rows, rows, rows, whole, whole]
            + [pl.BlockSpec((units, quarter), lambda i, me: (0, me[0])), block, block, block],
            out_specs=pl.BlockSpec((half, quarter), lambda i, me: (i, 0)),
        ),
        compiler_params=pltpu.CompilerParams(vmem_limit_bytes=60 << 20),
        cost_estimate=pl.CostEstimate(
            flops=8 * length * units * quarter, bytes_accessed=8 * units * (quarter + length) + 2 * length * quarter,
            transcendentals=0,
        ),
    )(me, own, last, following, top, bottom, w_down, w_last, w_next, w_far)


def shards(tokens, expert_ids, gate_codes, w_gate, w_up, w_down):
    groups = lax.axis_size("expert")
    parts = lax.axis_size("tensor")
    me = lax.axis_index("tensor")
    plane = lax.axis_index("expert") // PLANE
    planes = groups // PLANE
    rows, width = tokens.shape
    half, quarter = width // 2, width // parts
    units = w_gate.shape[2]
    in_plane = [[z * PLANE + j for j in range(PLANE)] for z in range(planes)]
    in_column = [[z * PLANE + j for z in range(planes)] for j in range(PLANE)]

    named = expert_ids[:, :, None] == jnp.arange(groups, dtype=jnp.int32)[None, None, :]
    member = jnp.any(named, axis=1)
    weight = jnp.sum(jnp.where(named, gate_codes[:, :, None], 0), axis=1).astype(jnp.float32) / 256.0
    earlier = (jnp.arange(rows)[:, None] > jnp.arange(rows)[None, :]).astype(jnp.bfloat16)
    slot = jnp.dot(earlier, member.astype(jnp.bfloat16), preferred_element_type=jnp.float32).astype(jnp.int32)
    slot = jnp.where(member, slot, -1).T
    weight = weight.T

    def ring(value, shift):
        return lax.ppermute(value, "expert", [(i, (i + shift * PLANE) % groups) for i in range(groups)])

    parity = lax.rem(me, 2)
    rings = []
    for part in range(2):
        mine = lax.dynamic_slice_in_dim(tokens, parity * half + part * quarter, quarter, 1)
        blocks = [mine] + [None] * (planes - 1)
        down = up = mine
        for step in range(1, planes // 2 + 1):
            if part and step > 1:
                down, up = after((down, up), rings[0][step - 1], rings[0][planes - step + 1])
            down = blocks[planes - step] = ring(down, 1)
            if 2 * step < planes:
                up = blocks[step] = ring(up, -1)
        rings.append(blocks)
    slots = lax.all_to_all(
        slot.reshape(planes, PLANE, rows), "expert", split_axis=0, concat_axis=0, tiled=True,
        axis_index_groups=in_column,
    )

    def columns_of(shift):
        return lax.dynamic_slice_in_dim(w_down[0], lax.rem(me + shift, parts) * quarter, quarter, 1)

    top = units // 2
    opposite = columns_of(2)
    down, up = both_ways(
        stack(columns_of(1), opposite[:top]), stack(columns_of(parts - 1), opposite[top:]), "tensor"
    )
    far = both_ways(down[units:], up[units:], "tensor")
    w_out = (w_down[0], down, up, stack(*far))

    def exchange(send):
        return lax.all_to_all(
            send, "expert", split_axis=0, concat_axis=0, tiled=True, axis_index_groups=in_plane
        )

    which = plane[None]
    got_a = exchange(select(which, slots, rings[:1], CHUNKS[:1])[0])
    got_b = exchange(after(select(which, slots, rings[1:], CHUNKS[:1])[0], got_a, down, up))
    sends = select(which, slots, rings, CHUNKS[1:])
    received = [(got_a, got_b)]
    arrived = [both_ways(got_a, after(got_b, *sends), "tensor")]
    last = got_b
    for send, passed in zip(sends, arrived[0]):
        last = exchange(after(send, last, passed, *far))
        received.append((last,))

    mixed = jnp.zeros((rows, quarter), jnp.float32)
    returned = None
    hiddens = []
    for step, (first, count) in enumerate(CHUNKS):
        own = received[step]
        if step:
            own = after(own, *arrived[step - 1])
            arrived.append(both_ways(own[0][:, :, :quarter], own[0][:, :, quarter:], "tensor"))
        hidden = hidden_of(which, parity[None], own, *arrived[step], w_gate[0], w_up[0], count)
        if step:
            hidden = after(hidden, *hiddens[step - 1][3:])
        hiddens.append(ring_gather(hidden, "tensor"))

    for step, (first, count) in enumerate(CHUNKS):
        out = down_of(me[None], hiddens[step], w_out).reshape(groups, count, quarter)
        out = after(out, last if returned is None else returned, *arrived[min(step + 1, len(CHUNKS) - 1)])
        returned = lax.all_to_all(out, "expert", split_axis=0, concat_axis=0, tiled=True)
        pick = slot[:, None, :] == (first + jnp.arange(count, dtype=jnp.int32))[None, :, None]
        scale = jnp.where(pick, weight[:, None, :], 0.0).astype(jnp.bfloat16).reshape(groups * count, rows)
        mixed = mixed + lax.dot_general(
            scale, returned.reshape(groups * count, quarter), (((0,), (0,)), ((), ())),
            preferred_element_type=jnp.float32,
        )
    return mixed.astype(jnp.bfloat16)


def solution(mesh):
    placed = (
        P("expert", None),
        P("expert", None),
        P("expert", None),
        P("expert", None, "tensor"),
        P("expert", None, "tensor"),
        P("expert", "tensor", None),
    )
    return jax.shard_map(
        shards, mesh=mesh, in_specs=placed, out_specs=P("expert", "tensor"), check_vma=False
    )
```

```python
import functools

import jax
import jax.numpy as jnp
from jax import lax
from jax.experimental import pallas as pl
from jax.experimental.pallas import tpu as pltpu
from jax.sharding import PartitionSpec as P

CHUNKS = ((0, 8), (8, 8), (16, 8))
PLANE = 8


def neighbours(shift, size):
    return [(i, (i + shift) % size) for i in range(size)]


def after(value, *earlier):
    return lax.optimization_barrier((value, earlier))[0]


def ring_gather(piece, axis, *first):
    size = lax.axis_size(axis)
    half = piece.shape[0] // 2
    last = lax.ppermute(piece, axis, neighbours(1, size))
    following = lax.ppermute(piece, axis, neighbours(-1, size))
    if first:
        last, following = after((last, following), *first)
    far_top = lax.ppermute(last[:half], axis, neighbours(1, size))
    far_bottom = lax.ppermute(following[half:], axis, neighbours(-1, size))
    return piece, last, following, far_top, far_bottom


def stack(*blocks):
    return jnp.concatenate(blocks, axis=0)


def both_ways(down, up, axis):
    size = lax.axis_size(axis)
    return (
        lax.ppermute(down, axis, neighbours(1, size)),
        lax.ppermute(up, axis, neighbours(-1, size)),
    )


def select_kernel(chunks, planes, plane_ref, slots_ref, *refs):
    outs = refs[-len(chunks):]
    parts = (len(refs) - len(outs)) // planes
    experts, length = slots_ref.shape[1:]
    for (first, count), out_ref in zip(chunks, outs):
        group = max(1, 16 // count)
        spot = lax.broadcasted_iota(jnp.int32, (experts, group * count, length), 1)
        for start in range(0, planes, group):
            picks = []
            for b in range(group):
                slot = slots_ref[lax.rem(plane_ref[0] + start + b, planes)] - first
                slot = jnp.where((slot >= 0) & (slot < count), slot + b * count, -1)
                pick = jnp.where(spot == slot[:, None, :], 1.0, 0.0).reshape(experts * group * count, length)
                picks.append(pick.astype(jnp.bfloat16))
            for part in range(parts):
                blocks = refs[part * planes + start:part * planes + start + group]
                width = blocks[0].shape[1]
                chosen = sum(jnp.dot(p, x[...], preferred_element_type=jnp.float32) for p, x in zip(picks, blocks))
                out_ref[:, start * count:(start + group) * count, part * width:(part + 1) * width] = (
                    chosen.astype(jnp.bfloat16).reshape(experts, group * count, width)
                )


def select(plane, slots, parts, chunks):
    planes, experts, length = slots.shape
    blocks = [block for part in parts for block in part]
    width = sum(part[0].shape[1] for part in parts)
    slots_out = sum(count for _, count in chunks) * planes * experts
    return pl.pallas_call(
        functools.partial(select_kernel, chunks, planes),
        out_shape=[jax.ShapeDtypeStruct((experts, planes * count, width), jnp.bfloat16) for _, count in chunks],
        grid_spec=pltpu.PrefetchScalarGridSpec(
            num_scalar_prefetch=1,
            grid=(1,),
            in_specs=[pl.BlockSpec(slots.shape, lambda i, plane: (0, 0, 0))]
            + [pl.BlockSpec(block.shape, lambda i, plane: (0, 0)) for block in blocks],
            out_specs=[
                pl.BlockSpec((experts, planes * count, width), lambda i, plane: (0, 0, 0)) for _, count in chunks
            ],
        ),
        compiler_params=pltpu.CompilerParams(vmem_limit_bytes=20 << 20),
        cost_estimate=pl.CostEstimate(
            flops=4 * slots_out * length * width, bytes_accessed=2 * width * (planes * length + slots_out),
            transcendentals=0,
        ),
    )(plane, slots, *blocks)


def hidden_kernel(inner, count, plane_ref, half_ref, own_ref, last_ref, next_ref, gate_ref, up_ref, out_ref, total):
    step = pl.program_id(0)
    outer, rows, width = own_ref.shape
    units = gate_ref.shape[1]

    def product(x_ref):
        w = jnp.concatenate([gate_ref[...], up_ref[...]], axis=1)
        return jnp.dot(x_ref[...].reshape(outer * rows, width), w, preferred_element_type=jnp.float32)

    @pl.when(step == 0)
    def _():
        total[...] = product(own_ref)

    @pl.when(step == 1)
    def _():
        total[...] += product(own_ref)

    @pl.when(step == 2)
    def _():
        total[...] += product(last_ref)

    @pl.when(step == 3)
    def _():
        both = total[...] + product(next_ref)
        gate, up = both[:, :units], both[:, units:]
        hidden = gate / (1.0 + jnp.exp(-gate)) * up
        for b in range(inner):
            block = jnp.concatenate(
                [hidden[j * rows + b * count:j * rows + (b + 1) * count] for j in range(outer)], axis=0
            )
            place = lax.rem(plane_ref[0] + b, inner) * (outer * count)
            out_ref[pl.ds(pl.multiple_of(place, outer * count), outer * count)] = block.astype(jnp.bfloat16)


def hidden_of(plane, parity, own, last, following, w_gate, w_up, count):
    outer, rows, quarter = last.shape
    units = w_gate.shape[1]
    weight = pl.BlockSpec((quarter, units), lambda k, plane, half: (lax.rem(half[0] * 2 + k, 4), 0))
    piece = pl.BlockSpec((outer, rows, quarter), lambda k, plane, half: (0, 0, 0))
    return pl.pallas_call(
        functools.partial(hidden_kernel, rows // count, count),
        out_shape=jax.ShapeDtypeStruct((outer * rows, units), jnp.bfloat16),
        grid_spec=pltpu.PrefetchScalarGridSpec(
            num_scalar_prefetch=2,
            grid=(4,),
            in_specs=[
                pl.BlockSpec((outer, rows, quarter), lambda k, plane, half: (0, 0, jnp.minimum(k, 1))),
                piece, piece, weight, weight,
            ],
            out_specs=pl.BlockSpec((outer * rows, units), lambda k, plane, half: (0, 0)),
            scratch_shapes=[pltpu.VMEM((outer * rows, 2 * units), jnp.float32)],
        ),
        compiler_params=pltpu.CompilerParams(vmem_limit_bytes=60 << 20),
        cost_estimate=pl.CostEstimate(
            flops=16 * outer * rows * quarter * units, bytes_accessed=8 * quarter * (outer * rows + 2 * units),
            transcendentals=outer * rows * units,
        ),
    )(plane, parity, own, last, following, w_gate, w_up)


def down_kernel(me_ref, own_ref, last_ref, next_ref, top_ref, bottom_ref, w_own, w_last, w_next, w_far, out_ref):
    total = jnp.dot(own_ref[...], w_own[...], preferred_element_type=jnp.float32)
    for x, w in ((last_ref, w_last), (next_ref, w_next)):
        total = total + jnp.dot(x[...], w[...], preferred_element_type=jnp.float32)
    far = [jnp.dot(x[...], w_far[...], preferred_element_type=jnp.float32) for x in (top_ref, bottom_ref)]
    out_ref[...] = (total + jnp.concatenate(far, axis=0)).astype(jnp.bfloat16)


def down_of(me, pieces, weights):
    own, last, following, top, bottom = pieces
    length, units = own.shape
    w_down, w_last, w_next, w_far = weights
    quarter = w_far.shape[1]
    steps = 4
    wide = quarter // steps
    rows = pl.BlockSpec((length, units), lambda i, me: (0, 0))
    half = pl.BlockSpec((length // 2, units), lambda i, me: (0, 0))
    block = pl.BlockSpec((units, wide), lambda i, me: (0, i))
    return pl.pallas_call(
        down_kernel,
        out_shape=jax.ShapeDtypeStruct((length, quarter), jnp.bfloat16),
        grid_spec=pltpu.PrefetchScalarGridSpec(
            num_scalar_prefetch=1,
            grid=(steps,),
            in_specs=[rows, rows, rows, half, half]
            + [pl.BlockSpec((units, wide), lambda i, me: (0, me[0] * steps + i)), block, block, block],
            out_specs=pl.BlockSpec((length, wide), lambda i, me: (0, i)),
        ),
        compiler_params=pltpu.CompilerParams(vmem_limit_bytes=60 << 20),
        cost_estimate=pl.CostEstimate(
            flops=8 * length * units * quarter, bytes_accessed=8 * units * (quarter + length) + 2 * length * quarter,
            transcendentals=0,
        ),
    )(me, own, last, following, top, bottom, w_down, w_last, w_next, w_far)


def shards(tokens, expert_ids, gate_codes, w_gate, w_up, w_down):
    groups = lax.axis_size("expert")
    parts = lax.axis_size("tensor")
    me = lax.axis_index("tensor")
    plane = lax.axis_index("expert") // PLANE
    planes = groups // PLANE
    rows, width = tokens.shape
    half, quarter = width // 2, width // parts
    units = w_gate.shape[2]
    in_plane = [[z * PLANE + j for j in range(PLANE)] for z in range(planes)]
    in_column = [[z * PLANE + j for z in range(planes)] for j in range(PLANE)]

    named = expert_ids[:, :, None] == jnp.arange(groups, dtype=jnp.int32)[None, None, :]
    member = jnp.any(named, axis=1)
    weight = jnp.sum(jnp.where(named, gate_codes[:, :, None], 0), axis=1).astype(jnp.float32) / 256.0
    earlier = (jnp.arange(rows)[:, None] > jnp.arange(rows)[None, :]).astype(jnp.bfloat16)
    slot = jnp.dot(earlier, member.astype(jnp.bfloat16), preferred_element_type=jnp.float32).astype(jnp.int32)
    slot = jnp.where(member, slot, -1).T
    weight = weight.T

    def ring(value, shift):
        return lax.ppermute(value, "expert", [(i, (i + shift * PLANE) % groups) for i in range(groups)])

    parity = lax.rem(me, 2)
    mine = lax.dynamic_slice_in_dim(tokens, parity * half, half, 1)
    blocks = [mine] + [None] * (planes - 1)
    down = up = mine
    for step in range(1, planes // 2 + 1):
        down = blocks[planes - step] = ring(down, 1)
        if 2 * step < planes:
            up = blocks[step] = ring(up, -1)
    slots = lax.all_to_all(
        slot.reshape(planes, PLANE, rows), "expert", split_axis=0, concat_axis=0, tiled=True,
        axis_index_groups=in_column,
    )

    def columns_of(shift):
        return lax.dynamic_slice_in_dim(w_down[0], lax.rem(me + shift, parts) * quarter, quarter, 1)

    top = units // 2
    opposite = columns_of(2)
    down, up = both_ways(
        stack(columns_of(1), opposite[:top]), stack(columns_of(parts - 1), opposite[top:]), "tensor"
    )
    far = both_ways(down[units:], up[units:], "tensor")
    w_out = (w_down[0], down, up, stack(*far))

    def exchange(send):
        return lax.all_to_all(
            send, "expert", split_axis=0, concat_axis=0, tiled=True, axis_index_groups=in_plane
        )

    which = plane[None]
    send = select(which, slots, [blocks], CHUNKS[:1])[0]
    sends = [send, *select(which, slots, [blocks], CHUNKS[1:])]
    received = []
    for step, send in enumerate(sends):
        if step == 1:
            send = after(send, *ends, down, up)
        elif step:
            send = after(send, received[-1], *far)
        got = exchange(send)
        if step == 0:
            got = after(got, *sends[1:])
            ends = [got[:, :, :quarter], got[:, :, quarter:]]
        received.append(got)

    mixed = jnp.zeros((rows, quarter), jnp.float32)
    returned = None
    arrived, firsts, hiddens, halves = [], [], [], []
    for step, (first, count) in enumerate(CHUNKS):
        own = received[step]
        if step:
            own = after(own, *arrived[step - 1])
            ends = [own[:, :, :quarter], own[:, :, quarter:]]
        halves.append(ends)
        arrived.append(both_ways(*ends, "tensor"))
        firsts.append(hidden_of(which, parity[None], own, *arrived[step], w_gate[0], w_up[0], count))
    for step, hidden in enumerate(firsts):
        if step:
            hidden = after(hidden, *hiddens[step - 1][3:])
        hiddens.append(ring_gather(hidden, "tensor", *received[step + 2:step + 3]))

    for step, (first, count) in enumerate(CHUNKS):
        out = down_of(me[None], hiddens[step], w_out).reshape(groups, count, quarter)
        out = after(out, received[-1] if returned is None else returned)
        if step + 1 < len(CHUNKS):
            out = after(out, firsts[step + 1], *(halves[step + 2] if step + 2 < len(CHUNKS) else ()))
        returned = lax.all_to_all(out, "expert", split_axis=0, concat_axis=0, tiled=True)
        pick = slot[:, None, :] == (first + jnp.arange(count, dtype=jnp.int32))[None, :, None]
        scale = jnp.where(pick, weight[:, None, :], 0.0).astype(jnp.bfloat16).reshape(groups * count, rows)
        mixed = mixed + lax.dot_general(
            scale, returned.reshape(groups * count, quarter), (((0,), (0,)), ((), ())),
            preferred_element_type=jnp.float32,
        )
    return mixed.astype(jnp.bfloat16)


def solution(mesh):
    placed = (
        P("expert", None),
        P("expert", None),
        P("expert", None),
        P("expert", None, "tensor"),
        P("expert", None, "tensor"),
        P("expert", "tensor", None),
    )
    return jax.shard_map(
        shards, mesh=mesh, in_specs=placed, out_specs=P("expert", "tensor"), check_vma=False
    )
```

```python
import functools

import jax
import jax.numpy as jnp
from jax import lax
from jax.experimental import pallas as pl
from jax.experimental.pallas import tpu as pltpu
from jax.sharding import PartitionSpec as P

CHUNKS = ((0, 8), (8, 8), (16, 8))
LIMIT = 60 << 20
PLANE = 8


def neighbours(shift, size):
    return [(i, (i + shift) % size) for i in range(size)]


def after(value, *earlier):
    return lax.optimization_barrier((value, earlier))[0]


def ring_gather(piece, axis):
    size = lax.axis_size(axis)
    half = piece.shape[0] // 2
    last = lax.ppermute(piece, axis, neighbours(1, size))
    following = lax.ppermute(piece, axis, neighbours(-1, size))
    far_top = lax.ppermute(last[:half], axis, neighbours(1, size))
    far_bottom = lax.ppermute(following[half:], axis, neighbours(-1, size))
    return piece, last, following, far_top, far_bottom


def stack(*blocks):
    return jnp.concatenate(blocks, axis=0)


def both_ways(down, up, axis):
    size = lax.axis_size(axis)
    return (
        lax.ppermute(down, axis, neighbours(1, size)),
        lax.ppermute(up, axis, neighbours(-1, size)),
    )


def select_kernel(chunks, planes, plane_ref, slots_ref, *refs):
    outs = refs[-len(chunks):]
    parts = (len(refs) - len(outs)) // planes
    experts, length = slots_ref.shape[1:]
    for (first, count), out_ref in zip(chunks, outs):
        group = max(1, 16 // count)
        spot = lax.broadcasted_iota(jnp.int32, (experts, group * count, length), 1)
        for start in range(0, planes, group):
            picks = []
            for b in range(group):
                slot = slots_ref[lax.rem(plane_ref[0] + start + b, planes)] - first
                slot = jnp.where((slot >= 0) & (slot < count), slot + b * count, -1)
                pick = jnp.where(spot == slot[:, None, :], 1.0, 0.0).reshape(experts * group * count, length)
                picks.append(pick.astype(jnp.bfloat16))
            for part in range(parts):
                blocks = refs[part * planes + start:part * planes + start + group]
                width = blocks[0].shape[1]
                chosen = sum(jnp.dot(p, x[...], preferred_element_type=jnp.float32) for p, x in zip(picks, blocks))
                out_ref[:, start * count:(start + group) * count, part * width:(part + 1) * width] = (
                    chosen.astype(jnp.bfloat16).reshape(experts, group * count, width)
                )


def select(plane, slots, parts, chunks):
    planes, experts, length = slots.shape
    blocks = [block for part in parts for block in part]
    width = sum(part[0].shape[1] for part in parts)
    slots_out = sum(count for _, count in chunks) * planes * experts
    return pl.pallas_call(
        functools.partial(select_kernel, chunks, planes),
        out_shape=[jax.ShapeDtypeStruct((experts, planes * count, width), jnp.bfloat16) for _, count in chunks],
        grid_spec=pltpu.PrefetchScalarGridSpec(
            num_scalar_prefetch=1,
            grid=(1,),
            in_specs=[pl.BlockSpec(slots.shape, lambda i, plane: (0, 0, 0))]
            + [pl.BlockSpec(block.shape, lambda i, plane: (0, 0)) for block in blocks],
            out_specs=[
                pl.BlockSpec((experts, planes * count, width), lambda i, plane: (0, 0, 0)) for _, count in chunks
            ],
        ),
        compiler_params=pltpu.CompilerParams(vmem_limit_bytes=20 << 20),
        cost_estimate=pl.CostEstimate(
            flops=4 * slots_out * length * width, bytes_accessed=2 * width * (planes * length + slots_out),
            transcendentals=0,
        ),
    )(plane, slots, *blocks)


def side_by_side(gate_ref, up_ref):
    return jnp.concatenate([gate_ref[...], up_ref[...]], axis=1)


def own_kernel(half_ref, own_ref, gate_ref, up_ref, out_ref):
    outer, rows, width = own_ref.shape
    x = own_ref[...].reshape(outer * rows, width)
    part = jnp.dot(x, side_by_side(gate_ref, up_ref), preferred_element_type=jnp.float32)

    @pl.when(pl.program_id(0) == 0)
    def _():
        out_ref[...] = part

    @pl.when(pl.program_id(0) > 0)
    def _():
        out_ref[...] += part


def own_part(parity, own, w_gate, w_up):
    outer, rows, half = own.shape
    units = w_gate.shape[1]
    quarter = half // 2
    weight = pl.BlockSpec((quarter, units), lambda k, half: (half[0] * 2 + k, 0))
    return pl.pallas_call(
        own_kernel,
        out_shape=jax.ShapeDtypeStruct((outer * rows, 2 * units), jnp.float32),
        grid_spec=pltpu.PrefetchScalarGridSpec(
            num_scalar_prefetch=1,
            grid=(2,),
            in_specs=[pl.BlockSpec((outer, rows, quarter), lambda k, half: (0, 0, k)), weight, weight],
            out_specs=pl.BlockSpec((outer * rows, 2 * units), lambda k, half: (0, 0)),
        ),
        compiler_params=pltpu.CompilerParams(vmem_limit_bytes=LIMIT),
        cost_estimate=pl.CostEstimate(
            flops=8 * outer * rows * quarter * units, bytes_accessed=14 << 20, transcendentals=0
        ),
    )(parity, own, w_gate, w_up)


def hidden_kernel(inner, count, plane_ref, half_ref, part_ref, last_ref, next_ref, gate_ref, up_ref, out_ref, total):
    outer, rows, width = last_ref.shape
    units = gate_ref.shape[1]

    def product(x_ref):
        x = x_ref[...].reshape(outer * rows, width)
        return jnp.dot(x, side_by_side(gate_ref, up_ref), preferred_element_type=jnp.float32)

    @pl.when(pl.program_id(0) == 0)
    def _():
        total[...] = part_ref[...] + product(last_ref)

    @pl.when(pl.program_id(0) == 1)
    def _():
        both = total[...] + product(next_ref)
        gate, up = both[:, :units], both[:, units:]
        hidden = gate / (1.0 + jnp.exp(-gate)) * up
        for b in range(inner):
            block = jnp.concatenate(
                [hidden[j * rows + b * count:j * rows + (b + 1) * count] for j in range(outer)], axis=0
            )
            place = lax.rem(plane_ref[0] + b, inner) * (outer * count)
            out_ref[pl.ds(pl.multiple_of(place, outer * count), outer * count)] = block.astype(jnp.bfloat16)


def hidden_of(plane, parity, part, last, following, w_gate, w_up, count):
    outer, rows, quarter = last.shape
    units = w_gate.shape[1]
    weight = pl.BlockSpec((quarter, units), lambda k, plane, half: (2 - 2 * half[0] + k, 0))
    piece = pl.BlockSpec((outer, rows, quarter), lambda k, plane, half: (0, 0, 0))
    return pl.pallas_call(
        functools.partial(hidden_kernel, rows // count, count),
        out_shape=jax.ShapeDtypeStruct((outer * rows, units), jnp.bfloat16),
        grid_spec=pltpu.PrefetchScalarGridSpec(
            num_scalar_prefetch=2,
            grid=(2,),
            in_specs=[
                pl.BlockSpec((outer * rows, 2 * units), lambda k, plane, half: (0, 0)), piece, piece, weight, weight
            ],
            out_specs=pl.BlockSpec((outer * rows, units), lambda k, plane, half: (0, 0)),
            scratch_shapes=[pltpu.VMEM((outer * rows, 2 * units), jnp.float32)],
        ),
        compiler_params=pltpu.CompilerParams(vmem_limit_bytes=LIMIT),
        cost_estimate=pl.CostEstimate(
            flops=8 * outer * rows * quarter * units, bytes_accessed=14 << 20, transcendentals=outer * rows * units
        ),
    )(plane, parity, part, last, following, w_gate, w_up)


def near_kernel(me_ref, own_ref, last_ref, next_ref, w_own, w_last, w_next, out_ref):
    out_ref[...] = sum(
        jnp.dot(x[...], w[...], preferred_element_type=jnp.float32)
        for x, w in ((own_ref, w_own), (last_ref, w_last), (next_ref, w_next))
    )


def near_part(me, pieces, weights):
    length, units = pieces[0].shape
    w_down, w_last, w_next, w_far = weights
    quarter = w_far.shape[1]
    steps = 2
    wide = quarter // steps
    rows = pl.BlockSpec((length, units), lambda i, me: (0, 0))
    block = pl.BlockSpec((units, wide), lambda i, me: (0, i))
    return pl.pallas_call(
        near_kernel,
        out_shape=jax.ShapeDtypeStruct((length, quarter), jnp.float32),
        grid_spec=pltpu.PrefetchScalarGridSpec(
            num_scalar_prefetch=1,
            grid=(steps,),
            in_specs=[rows] * 3
            + [pl.BlockSpec((units, wide), lambda i, me: (0, me[0] * steps + i)), block, block],
            out_specs=pl.BlockSpec((length, wide), lambda i, me: (0, i)),
        ),
        compiler_params=pltpu.CompilerParams(vmem_limit_bytes=LIMIT),
        cost_estimate=pl.CostEstimate(
            flops=6 * length * units * quarter, bytes_accessed=6 << 20, transcendentals=0
        ),
    )(me, *pieces, w_down, w_last, w_next)


def whole_kernel(part_ref, top_ref, bottom_ref, w_far, out_ref):
    x = jnp.concatenate([top_ref[...], bottom_ref[...]], axis=0)
    far = jnp.dot(x, w_far[...], preferred_element_type=jnp.float32)
    out_ref[...] = (part_ref[...] + far).astype(jnp.bfloat16)


def whole_of(part, top, bottom, w_far):
    length, quarter = part.shape
    units = w_far.shape[0]
    steps = 4
    wide = quarter // steps
    half = pl.BlockSpec((length // 2, units), lambda i: (0, 0))
    columns = pl.BlockSpec((length, wide), lambda i: (0, i))
    return pl.pallas_call(
        whole_kernel,
        out_shape=jax.ShapeDtypeStruct((length, quarter), jnp.bfloat16),
        grid=(steps,),
        in_specs=[columns, half, half, pl.BlockSpec((units, wide), lambda i: (0, i))],
        out_specs=columns,
        compiler_params=pltpu.CompilerParams(vmem_limit_bytes=LIMIT),
        cost_estimate=pl.CostEstimate(
            flops=2 * length * units * quarter, bytes_accessed=5 << 20, transcendentals=0
        ),
    )(part, top, bottom, w_far)


def shards(tokens, expert_ids, gate_codes, w_gate, w_up, w_down):
    groups = lax.axis_size("expert")
    parts = lax.axis_size("tensor")
    me = lax.axis_index("tensor")
    plane = lax.axis_index("expert") // PLANE
    planes = groups // PLANE
    rows, width = tokens.shape
    half, quarter = width // 2, width // parts
    units = w_gate.shape[2]
    in_plane = [[z * PLANE + j for j in range(PLANE)] for z in range(planes)]
    in_column = [[z * PLANE + j for z in range(planes)] for j in range(PLANE)]

    named = expert_ids[:, :, None] == jnp.arange(groups, dtype=jnp.int32)[None, None, :]
    member = jnp.any(named, axis=1)
    weight = jnp.sum(jnp.where(named, gate_codes[:, :, None], 0), axis=1).astype(jnp.float32) / 256.0
    earlier = (jnp.arange(rows)[:, None] > jnp.arange(rows)[None, :]).astype(jnp.bfloat16)
    slot = jnp.dot(earlier, member.astype(jnp.bfloat16), preferred_element_type=jnp.float32).astype(jnp.int32)
    slot = jnp.where(member, slot, -1).T
    weight = weight.T

    slots = lax.all_to_all(
        slot.reshape(planes, PLANE, rows), "expert", split_axis=0, concat_axis=0, tiled=True,
        axis_index_groups=in_column,
    )

    def ring(value, shift):
        return lax.ppermute(value, "expert", [(i, (i + shift * PLANE) % groups) for i in range(groups)])

    parity = lax.rem(me, 2)
    mine = lax.dynamic_slice_in_dim(tokens, parity * half, half, 1)
    blocks = [mine] + [None] * (planes - 1)
    down = up = mine
    for step in range(1, planes // 2 + 1):
        if step == 3:
            down, up = after((down, up), slots)
        down = blocks[planes - step] = ring(down, 1)
        if 2 * step < planes:
            up = blocks[step] = ring(up, -1)
    def columns_of(shift):
        return lax.dynamic_slice_in_dim(w_down[0], lax.rem(me + shift, parts) * quarter, quarter, 1)

    top = units // 2
    opposite = columns_of(2)
    down, up = both_ways(
        stack(columns_of(1), opposite[:top]), stack(columns_of(parts - 1), opposite[top:]), "tensor"
    )
    far = both_ways(down[units:], up[units:], "tensor")
    w_out = (w_down[0], down, up, stack(*far))

    def exchange(send):
        return lax.all_to_all(
            send, "expert", split_axis=0, concat_axis=0, tiled=True, axis_index_groups=in_plane
        )

    which = plane[None]
    send = select(which, slots, [blocks], CHUNKS[:1])[0]
    sends = [send, *select(which, slots, [blocks], CHUNKS[1:])]
    received, ends = [], []
    for step, send in enumerate(sends):
        send = after(send, *far) if step == 0 else after(send, received[-1], *(ends[0] if step == 1 else ()))
        got = exchange(send)
        if step == 0:
            got = after(got, *sends[1:])
        received.append(got)
        ends.append((got[:, :, :quarter], got[:, :, quarter:]))

    mixed = jnp.zeros((rows, quarter), jnp.float32)
    returned = None
    arrived, hiddens, parts_done = [], [], []
    for step, (first, count) in enumerate(CHUNKS):
        crossing = ends[step]
        if step:
            crossing = after(crossing, *arrived[step - 1])
            crossing = after(crossing, *hiddens[step - 1][1:3])
        arrived.append(both_ways(*crossing, "tensor"))
        part = own_part(parity[None], received[step], w_gate[0], w_up[0])
        parts_done.append(part)
        if step + 1 < len(CHUNKS):
            part = after(part, *ends[step + 1])
        hidden = hidden_of(which, parity[None], part, *arrived[step], w_gate[0], w_up[0], count)
        if step:
            hidden = after(hidden, *hiddens[step - 1][3:])
        hiddens.append(ring_gather(hidden, "tensor"))

    for step, (first, count) in enumerate(CHUNKS):
        part = near_part(me[None], hiddens[step][:3], w_out)
        out = whole_of(part, *hiddens[step][3:], w_out[3]).reshape(groups, count, quarter)
        out = after(out, received[-1] if returned is None else returned)
        if step == 1:
            out = after(out, *arrived[2], parts_done[2])
        returned = lax.all_to_all(out, "expert", split_axis=0, concat_axis=0, tiled=True)
        pick = slot[:, None, :] == (first + jnp.arange(count, dtype=jnp.int32))[None, :, None]
        scale = jnp.where(pick, weight[:, None, :], 0.0).astype(jnp.bfloat16).reshape(groups * count, rows)
        mixed = mixed + lax.dot_general(
            scale, returned.reshape(groups * count, quarter), (((0,), (0,)), ((), ())),
            preferred_element_type=jnp.float32,
        )
    return mixed.astype(jnp.bfloat16)


def solution(mesh):
    placed = (
        P("expert", None),
        P("expert", None),
        P("expert", None),
        P("expert", None, "tensor"),
        P("expert", None, "tensor"),
        P("expert", "tensor", None),
    )
    return jax.shard_map(
        shards, mesh=mesh, in_specs=placed, out_specs=P("expert", "tensor"), check_vma=False
    )
```

```python
import functools

import jax
import jax.numpy as jnp
from jax import lax
from jax.experimental import pallas as pl
from jax.experimental.pallas import tpu as pltpu
from jax.sharding import PartitionSpec as P

CHUNKS = ((0, 8), (8, 8), (16, 8))
PLANE = 8


def neighbours(shift, size):
    return [(i, (i + shift) % size) for i in range(size)]


def after(value, *earlier):
    return lax.optimization_barrier((value, earlier))[0]


def ring_gather(piece, axis, *first):
    size = lax.axis_size(axis)
    half = piece.shape[0] // 2
    last = lax.ppermute(piece, axis, neighbours(1, size))
    following = lax.ppermute(piece, axis, neighbours(-1, size))
    if first:
        last, following = after((last, following), *first)
    far_top = lax.ppermute(last[:half], axis, neighbours(1, size))
    far_bottom = lax.ppermute(following[half:], axis, neighbours(-1, size))
    return piece, last, following, far_top, far_bottom


def stack(*blocks):
    return jnp.concatenate(blocks, axis=0)


def both_ways(down, up, axis):
    size = lax.axis_size(axis)
    return (
        lax.ppermute(down, axis, neighbours(1, size)),
        lax.ppermute(up, axis, neighbours(-1, size)),
    )


def select_kernel(chunks, planes, plane_ref, slots_ref, *refs):
    outs = refs[-len(chunks):]
    parts = (len(refs) - len(outs)) // planes
    experts, length = slots_ref.shape[1:]
    for (first, count), out_ref in zip(chunks, outs):
        group = max(1, 16 // count)
        spot = lax.broadcasted_iota(jnp.int32, (experts, group * count, length), 1)
        for start in range(0, planes, group):
            picks = []
            for b in range(group):
                slot = slots_ref[lax.rem(plane_ref[0] + start + b, planes)] - first
                slot = jnp.where((slot >= 0) & (slot < count), slot + b * count, -1)
                pick = jnp.where(spot == slot[:, None, :], 1.0, 0.0).reshape(experts * group * count, length)
                picks.append(pick.astype(jnp.bfloat16))
            for part in range(parts):
                blocks = refs[part * planes + start:part * planes + start + group]
                width = blocks[0].shape[1]
                chosen = sum(jnp.dot(p, x[...], preferred_element_type=jnp.float32) for p, x in zip(picks, blocks))
                out_ref[:, start * count:(start + group) * count, part * width:(part + 1) * width] = (
                    chosen.astype(jnp.bfloat16).reshape(experts, group * count, width)
                )


def select(plane, slots, parts, chunks):
    planes, experts, length = slots.shape
    blocks = [block for part in parts for block in part]
    width = sum(part[0].shape[1] for part in parts)
    slots_out = sum(count for _, count in chunks) * planes * experts
    return pl.pallas_call(
        functools.partial(select_kernel, chunks, planes),
        out_shape=[jax.ShapeDtypeStruct((experts, planes * count, width), jnp.bfloat16) for _, count in chunks],
        grid_spec=pltpu.PrefetchScalarGridSpec(
            num_scalar_prefetch=1,
            grid=(1,),
            in_specs=[pl.BlockSpec(slots.shape, lambda i, plane: (0, 0, 0))]
            + [pl.BlockSpec(block.shape, lambda i, plane: (0, 0)) for block in blocks],
            out_specs=[
                pl.BlockSpec((experts, planes * count, width), lambda i, plane: (0, 0, 0)) for _, count in chunks
            ],
        ),
        compiler_params=pltpu.CompilerParams(vmem_limit_bytes=20 << 20),
        cost_estimate=pl.CostEstimate(
            flops=4 * slots_out * length * width, bytes_accessed=2 * width * (planes * length + slots_out),
            transcendentals=0,
        ),
    )(plane, slots, *blocks)


def hidden_kernel(inner, count, plane_ref, half_ref, own_ref, last_ref, next_ref, gate_ref, up_ref, out_ref, total):
    step = pl.program_id(0)
    outer, rows, width = own_ref.shape
    units = gate_ref.shape[1]

    def product(x_ref):
        w = jnp.concatenate([gate_ref[...], up_ref[...]], axis=1)
        return jnp.dot(x_ref[...].reshape(outer * rows, width), w, preferred_element_type=jnp.float32)

    @pl.when(step == 0)
    def _():
        total[...] = product(own_ref)

    @pl.when(step == 1)
    def _():
        total[...] += product(own_ref)

    @pl.when(step == 2)
    def _():
        total[...] += product(last_ref)

    @pl.when(step == 3)
    def _():
        both = total[...] + product(next_ref)
        gate, up = both[:, :units], both[:, units:]
        hidden = gate / (1.0 + jnp.exp(-gate)) * up
        for b in range(inner):
            block = jnp.concatenate(
                [hidden[j * rows + b * count:j * rows + (b + 1) * count] for j in range(outer)], axis=0
            )
            place = lax.rem(plane_ref[0] + b, inner) * (outer * count)
            out_ref[pl.ds(pl.multiple_of(place, outer * count), outer * count)] = block.astype(jnp.bfloat16)


def hidden_of(plane, parity, own, last, following, w_gate, w_up, count):
    outer, rows, quarter = last.shape
    units = w_gate.shape[1]
    weight = pl.BlockSpec((quarter, units), lambda k, plane, half: (lax.rem(half[0] * 2 + k, 4), 0))
    piece = pl.BlockSpec((outer, rows, quarter), lambda k, plane, half: (0, 0, 0))
    return pl.pallas_call(
        functools.partial(hidden_kernel, rows // count, count),
        out_shape=jax.ShapeDtypeStruct((outer * rows, units), jnp.bfloat16),
        grid_spec=pltpu.PrefetchScalarGridSpec(
            num_scalar_prefetch=2,
            grid=(4,),
            in_specs=[
                pl.BlockSpec((outer, rows, quarter), lambda k, plane, half: (0, 0, jnp.minimum(k, 1))),
                piece, piece, weight, weight,
            ],
            out_specs=pl.BlockSpec((outer * rows, units), lambda k, plane, half: (0, 0)),
            scratch_shapes=[pltpu.VMEM((outer * rows, 2 * units), jnp.float32)],
        ),
        compiler_params=pltpu.CompilerParams(vmem_limit_bytes=60 << 20),
        cost_estimate=pl.CostEstimate(
            flops=16 * outer * rows * quarter * units, bytes_accessed=8 * quarter * (outer * rows + 2 * units),
            transcendentals=outer * rows * units,
        ),
    )(plane, parity, own, last, following, w_gate, w_up)


def down_kernel(me_ref, own_ref, last_ref, next_ref, top_ref, bottom_ref, w_own, w_last, w_next, w_far, out_ref):
    def product(far_ref):
        total = jnp.dot(own_ref[...], w_own[...], preferred_element_type=jnp.float32)
        for x, w in ((last_ref, w_last), (next_ref, w_next), (far_ref, w_far)):
            total = total + jnp.dot(x[...], w[...], preferred_element_type=jnp.float32)
        out_ref[...] = total.astype(jnp.bfloat16)

    @pl.when(pl.program_id(0) == 0)
    def _():
        product(top_ref)

    @pl.when(pl.program_id(0) == 1)
    def _():
        product(bottom_ref)


def down_of(me, pieces, weights):
    own, last, following, top, bottom = pieces
    length, units = own.shape
    half = length // 2
    w_down, w_last, w_next, w_far = weights
    quarter = w_far.shape[1]
    rows = pl.BlockSpec((half, units), lambda i, me: (i, 0))
    whole = pl.BlockSpec((half, units), lambda i, me: (0, 0))
    block = pl.BlockSpec((units, quarter), lambda i, me: (0, 0))
    return pl.pallas_call(
        down_kernel,
        out_shape=jax.ShapeDtypeStruct((length, quarter), jnp.bfloat16),
        grid_spec=pltpu.PrefetchScalarGridSpec(
            num_scalar_prefetch=1,
            grid=(2,),
            in_specs=[rows, rows, rows, whole, whole]
            + [pl.BlockSpec((units, quarter), lambda i, me: (0, me[0])), block, block, block],
            out_specs=pl.BlockSpec((half, quarter), lambda i, me: (i, 0)),
        ),
        compiler_params=pltpu.CompilerParams(vmem_limit_bytes=32 << 20),
        cost_estimate=pl.CostEstimate(
            flops=8 * length * units * quarter, bytes_accessed=8 * units * (quarter + length) + 2 * length * quarter,
            transcendentals=0,
        ),
    )(me, own, last, following, top, bottom, w_down, w_last, w_next, w_far)


def shards(tokens, expert_ids, gate_codes, w_gate, w_up, w_down):
    groups = lax.axis_size("expert")
    parts = lax.axis_size("tensor")
    me = lax.axis_index("tensor")
    plane = lax.axis_index("expert") // PLANE
    planes = groups // PLANE
    rows, width = tokens.shape
    half, quarter = width // 2, width // parts
    units = w_gate.shape[2]
    in_plane = [[z * PLANE + j for j in range(PLANE)] for z in range(planes)]
    in_column = [[z * PLANE + j for z in range(planes)] for j in range(PLANE)]

    named = expert_ids[:, :, None] == jnp.arange(groups, dtype=jnp.int32)[None, None, :]
    member = jnp.any(named, axis=1)
    weight = jnp.sum(jnp.where(named, gate_codes[:, :, None], 0), axis=1).astype(jnp.float32) / 256.0
    earlier = (jnp.arange(rows)[:, None] > jnp.arange(rows)[None, :]).astype(jnp.bfloat16)
    slot = jnp.dot(earlier, member.astype(jnp.bfloat16), preferred_element_type=jnp.float32).astype(jnp.int32)
    slot = jnp.where(member, slot, -1).T
    weight = weight.T

    slots = lax.all_to_all(
        slot.reshape(planes, PLANE, rows), "expert", split_axis=0, concat_axis=0, tiled=True,
        axis_index_groups=in_column,
    )

    def ring(value, shift):
        return lax.ppermute(value, "expert", [(i, (i + shift * PLANE) % groups) for i in range(groups)])

    parity = lax.rem(me, 2)
    mine = lax.dynamic_slice_in_dim(tokens, parity * half, half, 1)
    blocks = [mine] + [None] * (planes - 1)
    down = up = mine
    for step in range(1, planes // 2 + 1):
        if 2 * step == planes:
            down = after(down, slots)
        down = blocks[planes - step] = ring(down, 1)
        if 2 * step < planes:
            up = blocks[step] = ring(up, -1)
    def columns_of(shift):
        return lax.dynamic_slice_in_dim(w_down[0], lax.rem(me + shift, parts) * quarter, quarter, 1)

    top = units // 2
    opposite = columns_of(2)
    down, up = both_ways(
        stack(columns_of(1), opposite[:top]), stack(columns_of(parts - 1), opposite[top:]), "tensor"
    )
    far = both_ways(down[units:], up[units:], "tensor")
    w_out = (w_down[0], down, up, stack(*far))

    def exchange(send):
        return lax.all_to_all(
            send, "expert", split_axis=0, concat_axis=0, tiled=True, axis_index_groups=in_plane
        )

    which = plane[None]
    send = select(which, slots, [blocks], CHUNKS[:1])[0]
    sends = [send, *select(which, slots, [blocks], CHUNKS[1:])]
    received, ends = [], []
    for step, send in enumerate(sends):
        send = after(send, *far) if step == 0 else after(send, received[-1], *(ends[0] if step == 1 else ()))
        got = exchange(send)
        if step == 0:
            got = after(got, *sends[1:])
        received.append(got)
        ends.append((got[:, :, :quarter], got[:, :, quarter:]))

    mixed = jnp.zeros((rows, quarter), jnp.float32)
    returned = None
    arrived, hiddens = [], []
    for step, (first, count) in enumerate(CHUNKS):
        crossing = ends[step]
        if step:
            crossing = after(crossing, *arrived[step - 1])
        if step >= 2:
            crossing = after(crossing, *hiddens[step - 2][3:])
        arrived.append(both_ways(*crossing, "tensor"))
        hidden = hidden_of(which, parity[None], received[step], *arrived[step], w_gate[0], w_up[0], count)
        if step:
            hidden = after(hidden, *hiddens[step - 1][3:])
        hiddens.append(ring_gather(hidden, "tensor", *(ends[step + 1] if step + 1 < len(CHUNKS) else ())))

    for step, (first, count) in enumerate(CHUNKS):
        out = down_of(me[None], hiddens[step], w_out).reshape(groups, count, quarter)
        out = after(out, received[-1] if returned is None else returned)
        returned = lax.all_to_all(out, "expert", split_axis=0, concat_axis=0, tiled=True)
        pick = slot[:, None, :] == (first + jnp.arange(count, dtype=jnp.int32))[None, :, None]
        scale = jnp.where(pick, weight[:, None, :], 0.0).astype(jnp.bfloat16).reshape(groups * count, rows)
        mixed = mixed + lax.dot_general(
            scale, returned.reshape(groups * count, quarter), (((0,), (0,)), ((), ())),
            preferred_element_type=jnp.float32,
        )
    return mixed.astype(jnp.bfloat16)


def solution(mesh):
    placed = (
        P("expert", None),
        P("expert", None),
        P("expert", None),
        P("expert", None, "tensor"),
        P("expert", None, "tensor"),
        P("expert", "tensor", None),
    )
    return jax.shard_map(
        shards, mesh=mesh, in_specs=placed, out_specs=P("expert", "tensor"), check_vma=False
    )
```

```python
import functools

import jax
import jax.numpy as jnp
from jax import lax
from jax.experimental import pallas as pl
from jax.experimental.pallas import tpu as pltpu
from jax.sharding import PartitionSpec as P

CHUNKS = ((0, 8), (8, 8), (16, 8))
PLANE = 8


def neighbours(shift, size):
    return [(i, (i + shift) % size) for i in range(size)]


def after(value, *earlier):
    return lax.optimization_barrier((value, earlier))[0]


def ring_gather(piece, axis, *first):
    size = lax.axis_size(axis)
    half = piece.shape[0] // 2
    last = lax.ppermute(piece, axis, neighbours(1, size))
    following = lax.ppermute(piece, axis, neighbours(-1, size))
    if first:
        last, following = after((last, following), *first)
    far_top = lax.ppermute(last[:half], axis, neighbours(1, size))
    far_bottom = lax.ppermute(following[half:], axis, neighbours(-1, size))
    return piece, last, following, far_top, far_bottom


def stack(*blocks):
    return jnp.concatenate(blocks, axis=0)


def both_ways(down, up, axis):
    size = lax.axis_size(axis)
    return (
        lax.ppermute(down, axis, neighbours(1, size)),
        lax.ppermute(up, axis, neighbours(-1, size)),
    )


def select_kernel(chunks, planes, plane_ref, slots_ref, *refs):
    outs = refs[-len(chunks):]
    parts = (len(refs) - len(outs)) // planes
    experts, length = slots_ref.shape[1:]
    for (first, count), out_ref in zip(chunks, outs):
        group = max(1, 16 // count)
        spot = lax.broadcasted_iota(jnp.int32, (experts, group * count, length), 1)
        for start in range(0, planes, group):
            picks = []
            for b in range(group):
                slot = slots_ref[lax.rem(plane_ref[0] + start + b, planes)] - first
                slot = jnp.where((slot >= 0) & (slot < count), slot + b * count, -1)
                pick = jnp.where(spot == slot[:, None, :], 1.0, 0.0).reshape(experts * group * count, length)
                picks.append(pick.astype(jnp.bfloat16))
            for part in range(parts):
                blocks = refs[part * planes + start:part * planes + start + group]
                width = blocks[0].shape[1]
                chosen = sum(jnp.dot(p, x[...], preferred_element_type=jnp.float32) for p, x in zip(picks, blocks))
                out_ref[:, start * count:(start + group) * count, part * width:(part + 1) * width] = (
                    chosen.astype(jnp.bfloat16).reshape(experts, group * count, width)
                )


def select(plane, slots, parts, chunks):
    planes, experts, length = slots.shape
    blocks = [block for part in parts for block in part]
    width = sum(part[0].shape[1] for part in parts)
    slots_out = sum(count for _, count in chunks) * planes * experts
    return pl.pallas_call(
        functools.partial(select_kernel, chunks, planes),
        out_shape=[jax.ShapeDtypeStruct((experts, planes * count, width), jnp.bfloat16) for _, count in chunks],
        grid_spec=pltpu.PrefetchScalarGridSpec(
            num_scalar_prefetch=1,
            grid=(1,),
            in_specs=[pl.BlockSpec(slots.shape, lambda i, plane: (0, 0, 0))]
            + [pl.BlockSpec(block.shape, lambda i, plane: (0, 0)) for block in blocks],
            out_specs=[
                pl.BlockSpec((experts, planes * count, width), lambda i, plane: (0, 0, 0)) for _, count in chunks
            ],
        ),
        compiler_params=pltpu.CompilerParams(vmem_limit_bytes=20 << 20),
        cost_estimate=pl.CostEstimate(
            flops=4 * slots_out * length * width, bytes_accessed=2 * width * (planes * length + slots_out),
            transcendentals=0,
        ),
    )(plane, slots, *blocks)


def hidden_kernel(inner, count, plane_ref, half_ref, own_ref, *refs):
    step = pl.program_id(0)
    *sides, gate_ref, up_ref, out_ref, total = refs
    cuts = len(sides) // 2
    outer, rows, width = own_ref.shape
    units = gate_ref.shape[1]

    def product(*x_refs):
        w = jnp.concatenate([gate_ref[...], up_ref[...]], axis=1)
        x = x_refs[0][...] if len(x_refs) == 1 else jnp.concatenate([x[...] for x in x_refs], axis=1)
        return jnp.dot(x.reshape(outer * rows, width), w, preferred_element_type=jnp.float32)

    @pl.when(step == 0)
    def _():
        total[...] = product(own_ref)

    @pl.when(step == 1)
    def _():
        total[...] += product(own_ref)

    @pl.when(step == 2)
    def _():
        total[...] += product(*sides[:cuts])

    @pl.when(step == 3)
    def _():
        both = total[...] + product(*sides[cuts:])
        gate, up = both[:, :units], both[:, units:]
        hidden = gate / (1.0 + jnp.exp(-gate)) * up
        for b in range(inner):
            block = jnp.concatenate(
                [hidden[j * rows + b * count:j * rows + (b + 1) * count] for j in range(outer)], axis=0
            )
            place = lax.rem(plane_ref[0] + b, inner) * (outer * count)
            out_ref[pl.ds(pl.multiple_of(place, outer * count), outer * count)] = block.astype(jnp.bfloat16)


def hidden_of(plane, parity, own, last, following, w_gate, w_up, count):
    outer, rows, half = own.shape
    quarter = half // 2
    sides = [*last, *following]
    units = w_gate.shape[1]
    weight = pl.BlockSpec((quarter, units), lambda k, plane, half: (lax.rem(half[0] * 2 + k, 4), 0))
    pieces = [pl.BlockSpec(side.shape, lambda k, plane, half: (0, 0, 0)) for side in sides]
    return pl.pallas_call(
        functools.partial(hidden_kernel, rows // count, count),
        out_shape=jax.ShapeDtypeStruct((outer * rows, units), jnp.bfloat16),
        grid_spec=pltpu.PrefetchScalarGridSpec(
            num_scalar_prefetch=2,
            grid=(4,),
            in_specs=[
                pl.BlockSpec((outer, rows, quarter), lambda k, plane, half: (0, 0, jnp.minimum(k, 1))),
                *pieces, weight, weight,
            ],
            out_specs=pl.BlockSpec((outer * rows, units), lambda k, plane, half: (0, 0)),
            scratch_shapes=[pltpu.VMEM((outer * rows, 2 * units), jnp.float32)],
        ),
        compiler_params=pltpu.CompilerParams(vmem_limit_bytes=60 << 20),
        cost_estimate=pl.CostEstimate(
            flops=16 * outer * rows * quarter * units, bytes_accessed=8 * quarter * (outer * rows + 2 * units),
            transcendentals=outer * rows * units,
        ),
    )(plane, parity, own, *sides, w_gate, w_up)


def down_kernel(me_ref, own_ref, last_ref, next_ref, top_ref, bottom_ref, w_own, w_last, w_next, w_far, out_ref):
    def product(far_ref):
        total = jnp.dot(own_ref[...], w_own[...], preferred_element_type=jnp.float32)
        for x, w in ((last_ref, w_last), (next_ref, w_next), (far_ref, w_far)):
            total = total + jnp.dot(x[...], w[...], preferred_element_type=jnp.float32)
        out_ref[...] = total.astype(jnp.bfloat16)

    @pl.when(pl.program_id(0) == 0)
    def _():
        product(top_ref)

    @pl.when(pl.program_id(0) == 1)
    def _():
        product(bottom_ref)


def down_of(me, pieces, weights):
    own, last, following, top, bottom = pieces
    length, units = own.shape
    half = length // 2
    w_down, w_last, w_next, w_far = weights
    quarter = w_far.shape[1]
    rows = pl.BlockSpec((half, units), lambda i, me: (i, 0))
    whole = pl.BlockSpec((half, units), lambda i, me: (0, 0))
    block = pl.BlockSpec((units, quarter), lambda i, me: (0, 0))
    return pl.pallas_call(
        down_kernel,
        out_shape=jax.ShapeDtypeStruct((length, quarter), jnp.bfloat16),
        grid_spec=pltpu.PrefetchScalarGridSpec(
            num_scalar_prefetch=1,
            grid=(2,),
            in_specs=[rows, rows, rows, whole, whole]
            + [pl.BlockSpec((units, quarter), lambda i, me: (0, me[0])), block, block, block],
            out_specs=pl.BlockSpec((half, quarter), lambda i, me: (i, 0)),
        ),
        compiler_params=pltpu.CompilerParams(vmem_limit_bytes=32 << 20),
        cost_estimate=pl.CostEstimate(
            flops=8 * length * units * quarter, bytes_accessed=8 * units * (quarter + length) + 2 * length * quarter,
            transcendentals=0,
        ),
    )(me, own, last, following, top, bottom, w_down, w_last, w_next, w_far)


def shards(tokens, expert_ids, gate_codes, w_gate, w_up, w_down):
    groups = lax.axis_size("expert")
    parts = lax.axis_size("tensor")
    me = lax.axis_index("tensor")
    plane = lax.axis_index("expert") // PLANE
    planes = groups // PLANE
    rows, width = tokens.shape
    half, quarter = width // 2, width // parts
    units = w_gate.shape[2]
    in_plane = [[z * PLANE + j for j in range(PLANE)] for z in range(planes)]
    in_column = [[z * PLANE + j for z in range(planes)] for j in range(PLANE)]

    named = expert_ids[:, :, None] == jnp.arange(groups, dtype=jnp.int32)[None, None, :]
    member = jnp.any(named, axis=1)
    weight = jnp.sum(jnp.where(named, gate_codes[:, :, None], 0), axis=1).astype(jnp.float32) / 256.0
    earlier = (jnp.arange(rows)[:, None] > jnp.arange(rows)[None, :]).astype(jnp.bfloat16)
    slot = jnp.dot(earlier, member.astype(jnp.bfloat16), preferred_element_type=jnp.float32).astype(jnp.int32)
    slot = jnp.where(member, slot, -1).T
    weight = weight.T

    slots = lax.all_to_all(
        slot.reshape(planes, PLANE, rows), "expert", split_axis=0, concat_axis=0, tiled=True,
        axis_index_groups=in_column,
    )

    def ring(value, shift):
        return lax.ppermute(value, "expert", [(i, (i + shift * PLANE) % groups) for i in range(groups)])

    parity = lax.rem(me, 2)
    mine = lax.dynamic_slice_in_dim(tokens, parity * half, half, 1)
    blocks = [mine] + [None] * (planes - 1)
    down = up = mine
    for step in range(1, planes // 2 + 1):
        if 2 * step == planes:
            down = after(down, slots)
        down = blocks[planes - step] = ring(down, 1)
        if 2 * step < planes:
            up = blocks[step] = ring(up, -1)
    def columns_of(shift):
        return lax.dynamic_slice_in_dim(w_down[0], lax.rem(me + shift, parts) * quarter, quarter, 1)

    top = units // 2
    opposite = columns_of(2)
    down, up = both_ways(
        stack(columns_of(1), opposite[:top]), stack(columns_of(parts - 1), opposite[top:]), "tensor"
    )
    far = both_ways(down[units:], up[units:], "tensor")
    w_out = (w_down[0], down, up, stack(*far))

    def exchange(send):
        return lax.all_to_all(
            send, "expert", split_axis=0, concat_axis=0, tiled=True, axis_index_groups=in_plane
        )

    which = plane[None]
    send = select(which, slots, [blocks], CHUNKS[:1])[0]
    sends = [send, *select(which, slots, [blocks], CHUNKS[1:])]
    received, ends = [], []
    for step, send in enumerate(sends):
        send = after(send, *far) if step == 0 else after(send, received[-1], *(ends[0] if step == 1 else ()))
        got = exchange(send)
        if step == 0:
            got = after(got, *sends[1:])
        received.append(got)
        ends.append((got[:, :, :quarter], got[:, :, quarter:]))

    mixed = jnp.zeros((rows, quarter), jnp.float32)
    returned = None
    arrived, hiddens, products = [], [], []
    final = len(CHUNKS) - 1
    early = both_ways(*after(ends[final], *ends[final - 1]), "tensor")
    for step, (first, count) in enumerate(CHUNKS):
        if step < final:
            crossing = ends[step] if step == 0 else after(ends[step], *arrived[step - 1])
            arrived.append(both_ways(*crossing, "tensor"))
        else:
            arrived.append(early)
        sides = [(side,) for side in arrived[step]]
        hidden = hidden_of(which, parity[None], received[step], *sides, w_gate[0], w_up[0], count)
        products.append(hidden)
        if step:
            hidden = after(hidden, *hiddens[step - 1][3:])
        hold = () if step == final else ends[step + 1] if step + 1 < final else early
        hiddens.append(ring_gather(hidden, "tensor", *hold))

    for step, (first, count) in enumerate(CHUNKS):
        out = down_of(me[None], hiddens[step], w_out).reshape(groups, count, quarter)
        out = after(out, received[-1] if returned is None else returned)
        if step + 1 == final:
            out = after(out, products[final])
        returned = lax.all_to_all(out, "expert", split_axis=0, concat_axis=0, tiled=True)
        pick = slot[:, None, :] == (first + jnp.arange(count, dtype=jnp.int32))[None, :, None]
        scale = jnp.where(pick, weight[:, None, :], 0.0).astype(jnp.bfloat16).reshape(groups * count, rows)
        mixed = mixed + lax.dot_general(
            scale, returned.reshape(groups * count, quarter), (((0,), (0,)), ((), ())),
            preferred_element_type=jnp.float32,
        )
        if step + 1 < len(CHUNKS):
            mixed = lax.optimization_barrier(mixed)
    return mixed.astype(jnp.bfloat16)


def solution(mesh):
    placed = (
        P("expert", None),
        P("expert", None),
        P("expert", None),
        P("expert", None, "tensor"),
        P("expert", None, "tensor"),
        P("expert", "tensor", None),
    )
    return jax.shard_map(
        shards, mesh=mesh, in_specs=placed, out_specs=P("expert", "tensor"), check_vma=False
    )
```

```python
import functools

import jax
import jax.numpy as jnp
from jax import lax
from jax.experimental import pallas as pl
from jax.experimental.pallas import tpu as pltpu
from jax.sharding import PartitionSpec as P

CHUNKS = ((0, 8), (8, 8), (16, 8))
PLANE = 8


def neighbours(shift, size):
    return [(i, (i + shift) % size) for i in range(size)]


def after(value, *earlier):
    return lax.optimization_barrier((value, earlier))[0]


def ring_gather(piece, axis, *first):
    size = lax.axis_size(axis)
    half = piece.shape[0] // 2
    last = lax.ppermute(piece, axis, neighbours(1, size))
    following = lax.ppermute(piece, axis, neighbours(-1, size))
    if first:
        last, following = after((last, following), *first)
    far_top = lax.ppermute(last[:half], axis, neighbours(1, size))
    far_bottom = lax.ppermute(following[half:], axis, neighbours(-1, size))
    return piece, last, following, far_top, far_bottom


def stack(*blocks):
    return jnp.concatenate(blocks, axis=0)


def both_ways(down, up, axis):
    size = lax.axis_size(axis)
    return (
        lax.ppermute(down, axis, neighbours(1, size)),
        lax.ppermute(up, axis, neighbours(-1, size)),
    )


def select_kernel(chunks, planes, plane_ref, slots_ref, *refs):
    outs = refs[-len(chunks):]
    parts = (len(refs) - len(outs)) // planes
    experts, length = slots_ref.shape[1:]
    for (first, count), out_ref in zip(chunks, outs):
        group = max(1, 16 // count)
        spot = lax.broadcasted_iota(jnp.int32, (experts, group * count, length), 1)
        for start in range(0, planes, group):
            picks = []
            for b in range(group):
                slot = slots_ref[lax.rem(plane_ref[0] + start + b, planes)] - first
                slot = jnp.where((slot >= 0) & (slot < count), slot + b * count, -1)
                pick = jnp.where(spot == slot[:, None, :], 1.0, 0.0).reshape(experts * group * count, length)
                picks.append(pick.astype(jnp.bfloat16))
            for part in range(parts):
                blocks = refs[part * planes + start:part * planes + start + group]
                width = blocks[0].shape[1]
                chosen = sum(jnp.dot(p, x[...], preferred_element_type=jnp.float32) for p, x in zip(picks, blocks))
                out_ref[:, start * count:(start + group) * count, part * width:(part + 1) * width] = (
                    chosen.astype(jnp.bfloat16).reshape(experts, group * count, width)
                )


def select(plane, slots, parts, chunks):
    planes, experts, length = slots.shape
    blocks = [block for part in parts for block in part]
    width = sum(part[0].shape[1] for part in parts)
    slots_out = sum(count for _, count in chunks) * planes * experts
    return pl.pallas_call(
        functools.partial(select_kernel, chunks, planes),
        out_shape=[jax.ShapeDtypeStruct((experts, planes * count, width), jnp.bfloat16) for _, count in chunks],
        grid_spec=pltpu.PrefetchScalarGridSpec(
            num_scalar_prefetch=1,
            grid=(1,),
            in_specs=[pl.BlockSpec(slots.shape, lambda i, plane: (0, 0, 0))]
            + [pl.BlockSpec(block.shape, lambda i, plane: (0, 0)) for block in blocks],
            out_specs=[
                pl.BlockSpec((experts, planes * count, width), lambda i, plane: (0, 0, 0)) for _, count in chunks
            ],
        ),
        compiler_params=pltpu.CompilerParams(vmem_limit_bytes=20 << 20),
        cost_estimate=pl.CostEstimate(
            flops=4 * slots_out * length * width, bytes_accessed=2 * width * (planes * length + slots_out),
            transcendentals=0,
        ),
    )(plane, slots, *blocks)


def hidden_kernel(inner, count, plane_ref, half_ref, own_ref, last_ref, next_ref, gate_ref, up_ref, out_ref, total):
    step = pl.program_id(0)
    outer, rows, width = own_ref.shape
    units = gate_ref.shape[1]

    def product(x_ref):
        w = jnp.concatenate([gate_ref[...], up_ref[...]], axis=1)
        return jnp.dot(x_ref[...].reshape(outer * rows, width), w, preferred_element_type=jnp.float32)

    @pl.when(step == 0)
    def _():
        total[...] = product(own_ref)

    @pl.when(step == 1)
    def _():
        total[...] += product(own_ref)

    @pl.when(step == 2)
    def _():
        total[...] += product(last_ref)

    @pl.when(step == 3)
    def _():
        both = total[...] + product(next_ref)
        gate, up = both[:, :units], both[:, units:]
        hidden = gate / (1.0 + jnp.exp(-gate)) * up
        for b in range(inner):
            block = jnp.concatenate(
                [hidden[j * rows + b * count:j * rows + (b + 1) * count] for j in range(outer)], axis=0
            )
            place = lax.rem(plane_ref[0] + b, inner) * (outer * count)
            out_ref[pl.ds(pl.multiple_of(place, outer * count), outer * count)] = block.astype(jnp.bfloat16)


def hidden_of(plane, parity, own, last, following, w_gate, w_up, count):
    outer, rows, quarter = last.shape
    units = w_gate.shape[1]
    weight = pl.BlockSpec((quarter, units), lambda k, plane, half: (lax.rem(half[0] * 2 + k, 4), 0))
    piece = pl.BlockSpec((outer, rows, quarter), lambda k, plane, half: (0, 0, 0))
    return pl.pallas_call(
        functools.partial(hidden_kernel, rows // count, count),
        out_shape=jax.ShapeDtypeStruct((outer * rows, units), jnp.bfloat16),
        grid_spec=pltpu.PrefetchScalarGridSpec(
            num_scalar_prefetch=2,
            grid=(4,),
            in_specs=[
                pl.BlockSpec((outer, rows, quarter), lambda k, plane, half: (0, 0, jnp.minimum(k, 1))),
                piece, piece, weight, weight,
            ],
            out_specs=pl.BlockSpec((outer * rows, units), lambda k, plane, half: (0, 0)),
            scratch_shapes=[pltpu.VMEM((outer * rows, 2 * units), jnp.float32)],
        ),
        compiler_params=pltpu.CompilerParams(vmem_limit_bytes=60 << 20),
        cost_estimate=pl.CostEstimate(
            flops=16 * outer * rows * quarter * units, bytes_accessed=8 * quarter * (outer * rows + 2 * units),
            transcendentals=outer * rows * units,
        ),
    )(plane, parity, own, last, following, w_gate, w_up)


def down_kernel(me_ref, own_ref, last_ref, next_ref, top_ref, bottom_ref, w_own, w_last, w_next, w_far, out_ref):
    def product(far_ref):
        total = jnp.dot(own_ref[...], w_own[...], preferred_element_type=jnp.float32)
        for x, w in ((last_ref, w_last), (next_ref, w_next), (far_ref, w_far)):
            total = total + jnp.dot(x[...], w[...], preferred_element_type=jnp.float32)
        out_ref[...] = total.astype(jnp.bfloat16)

    @pl.when(pl.program_id(0) == 0)
    def _():
        product(top_ref)

    @pl.when(pl.program_id(0) == 1)
    def _():
        product(bottom_ref)


def down_of(me, pieces, weights):
    own, last, following, top, bottom = pieces
    length, units = own.shape
    half = length // 2
    w_down, w_last, w_next, w_far = weights
    quarter = w_far.shape[1]
    rows = pl.BlockSpec((half, units), lambda i, me: (i, 0))
    whole = pl.BlockSpec((half, units), lambda i, me: (0, 0))
    block = pl.BlockSpec((units, quarter), lambda i, me: (0, 0))
    return pl.pallas_call(
        down_kernel,
        out_shape=jax.ShapeDtypeStruct((length, quarter), jnp.bfloat16),
        grid_spec=pltpu.PrefetchScalarGridSpec(
            num_scalar_prefetch=1,
            grid=(2,),
            in_specs=[rows, rows, rows, whole, whole]
            + [pl.BlockSpec((units, quarter), lambda i, me: (0, me[0])), block, block, block],
            out_specs=pl.BlockSpec((half, quarter), lambda i, me: (i, 0)),
        ),
        compiler_params=pltpu.CompilerParams(vmem_limit_bytes=32 << 20),
        cost_estimate=pl.CostEstimate(
            flops=8 * length * units * quarter, bytes_accessed=8 * units * (quarter + length) + 2 * length * quarter,
            transcendentals=0,
        ),
    )(me, own, last, following, top, bottom, w_down, w_last, w_next, w_far)


def shards(tokens, expert_ids, gate_codes, w_gate, w_up, w_down):
    groups = lax.axis_size("expert")
    parts = lax.axis_size("tensor")
    me = lax.axis_index("tensor")
    plane = lax.axis_index("expert") // PLANE
    planes = groups // PLANE
    rows, width = tokens.shape
    half, quarter = width // 2, width // parts
    units = w_gate.shape[2]
    in_plane = [[z * PLANE + j for j in range(PLANE)] for z in range(planes)]
    in_column = [[z * PLANE + j for z in range(planes)] for j in range(PLANE)]

    named = expert_ids[:, :, None] == jnp.arange(groups, dtype=jnp.int32)[None, None, :]
    member = jnp.any(named, axis=1)
    weight = jnp.sum(jnp.where(named, gate_codes[:, :, None], 0), axis=1).astype(jnp.float32) / 256.0
    earlier = (jnp.arange(rows)[:, None] > jnp.arange(rows)[None, :]).astype(jnp.bfloat16)
    slot = jnp.dot(earlier, member.astype(jnp.bfloat16), preferred_element_type=jnp.float32).astype(jnp.int32)
    slot = jnp.where(member, slot, -1).T
    weight = weight.T

    slots = lax.all_to_all(
        slot.reshape(planes, PLANE, rows), "expert", split_axis=0, concat_axis=0, tiled=True,
        axis_index_groups=in_column,
    )

    def ring(value, shift):
        return lax.ppermute(value, "expert", [(i, (i + shift * PLANE) % groups) for i in range(groups)])

    parity = lax.rem(me, 2)
    mine = lax.dynamic_slice_in_dim(tokens, parity * half, half, 1)
    blocks = [mine] + [None] * (planes - 1)
    down = up = mine
    for step in range(1, planes // 2 + 1):
        if 2 * step == planes:
            down = after(down, slots)
        down = blocks[planes - step] = ring(down, 1)
        if 2 * step < planes:
            up = blocks[step] = ring(up, -1)
    def columns_of(shift):
        return lax.dynamic_slice_in_dim(w_down[0], lax.rem(me + shift, parts) * quarter, quarter, 1)

    top = units // 2
    opposite = columns_of(2)
    down, up = both_ways(
        stack(columns_of(1), opposite[:top]), stack(columns_of(parts - 1), opposite[top:]), "tensor"
    )
    far = both_ways(down[units:], up[units:], "tensor")
    w_out = (w_down[0], down, up, stack(*far))

    def exchange(send):
        return lax.all_to_all(
            send, "expert", split_axis=0, concat_axis=0, tiled=True, axis_index_groups=in_plane
        )

    which = plane[None]
    send = select(which, slots, [blocks], CHUNKS[:1])[0]
    sends = [send, *select(which, slots, [blocks], CHUNKS[1:])]
    received, ends = [], []
    for step, send in enumerate(sends):
        send = after(send, *far) if step == 0 else after(send, received[-1], *(ends[0] if step == 1 else ()))
        got = exchange(send)
        if step == 0:
            got = after(got, *sends[1:])
        received.append(got)
        ends.append((got[:, :, :quarter], got[:, :, quarter:]))

    mixed = jnp.zeros((rows, quarter), jnp.float32)
    returned = None
    arrived, hiddens = [], []
    for step, (first, count) in enumerate(CHUNKS):
        crossing = ends[step]
        if step:
            crossing = after(crossing, *arrived[step - 1])
        if step >= 2:
            crossing = after(crossing, *hiddens[step - 2][3:])
        arrived.append(both_ways(*crossing, "tensor"))
        hidden = hidden_of(which, parity[None], received[step], *arrived[step], w_gate[0], w_up[0], count)
        if step:
            hidden = after(hidden, *hiddens[step - 1][3:])
        hiddens.append(ring_gather(hidden, "tensor", *(ends[step + 1] if step + 1 < len(CHUNKS) else ())))

    for step, (first, count) in enumerate(CHUNKS):
        out = down_of(me[None], hiddens[step], w_out).reshape(groups, count, quarter)
        out = after(out, received[-1] if returned is None else returned)
        returned = lax.all_to_all(out, "expert", split_axis=0, concat_axis=0, tiled=True)
        pick = slot[:, None, :] == (first + jnp.arange(count, dtype=jnp.int32))[None, :, None]
        scale = jnp.where(pick, weight[:, None, :], 0.0).astype(jnp.bfloat16).reshape(groups * count, rows)
        mixed = mixed + lax.dot_general(
            scale, returned.reshape(groups * count, quarter), (((0,), (0,)), ((), ())),
            preferred_element_type=jnp.float32,
        )
        if step + 1 < len(CHUNKS):
            mixed = lax.optimization_barrier(mixed)
    return mixed.astype(jnp.bfloat16)


def solution(mesh):
    placed = (
        P("expert", None),
        P("expert", None),
        P("expert", None),
        P("expert", None, "tensor"),
        P("expert", None, "tensor"),
        P("expert", "tensor", None),
    )
    return jax.shard_map(
        shards, mesh=mesh, in_specs=placed, out_specs=P("expert", "tensor"), check_vma=False
    )
```
